32 devices in a mesh: tm: 4 (over y, x), det: 8 (over z, core).
Axes of the slice: x: 2, y: 2, z: 4, core: 2. Of those that a mesh axis runs over, the one named last changes fastest.
Arguments:
- timestream: float32 [4, 128, 8192], P('tm', 'det'), may hold values from -0.8 to 0.8
- polar_angle: float32 [4, 128, 8192], P('tm', 'det'), may hold values from -3.140625 to 3.140625
- pixel_index: int32 [4, 128, 8192], P('tm', 'det'), may hold values from 0 to 2047
- strip_tile: int32 [4, 128, 64], P('tm', 'det'), may hold values from 0 to 7
- time_const: float32 [4, 128], P('tm', 'det'), may hold values from 0.2 to 2
- knee_freq: float32 [4, 128], P('tm', 'det'), may hold values from 0.005 to 0.05
- noise_slope: float32 [4, 128], P('tm', 'det'), may hold values from 1 to 3
- white_weight: float32 [4, 128], P('tm', 'det'), may hold values from 0.5 to 2
- mode_mix: float32 [4, 128, 64], P('tm', 'det'), may hold values from -1 to 1
- coupling: float32 [64, 64], replicated, may hold values from -1 to 2
- device_slots: int32 [4, 64], P('tm', 'det'), may hold values from 0 to 31, as said below
- slot_home: int32 [4, 32], P('tm', 'det'), may hold values from 0 to 31, as said below
Outputs:
- sky_map: float32 [256, 3, 2048], P(('tm', 'det'))
The draws below stay inside these ranges and needn't reach their ends.
Inputs may be any that keep to these rules, and one draw needn't show every extreme that they name: `device_slots`: entries j * 8 to (j + 1) * 8 - 1 of a row are the entries of the group's tile list that device j of the group touches, all distinct. Of each block of 4 entries (those with the same entry // 4) a device touches exactly 2 in half of the blocks and exactly 0 in the others. `slot_home`: entry s of group g is owner_tm * 8 + place: the tile is held at place place by the device with tm index owner_tm and det index s // 4. Entries of one block of 4 are distinct; in every block exactly 2 entries share one owner_tm, and the others are spread as evenly as possible over the other owner_tm values.
All inputs are finite; a program needn't handle non-finite values.
Results may differ from the reference program's by a relative error of at most 0.0001.
Values sent between devices are 32-bit elements; how exact they have to be, the bound alone decides.
A program may use at most 64 MiB of HBM per device.

```python
import math
import jax
import jax.numpy as jnp
from jax import lax

SAMPLES = 4096
SCANS = 2
STRIP = 128
TILE_PIX = 2048
MODES = 64
DET_DEV = 16
GSHARE = 4
TOUCH = 1
CAPD = 2
CAPT = 2
OWN = 8
DETS = 128
STRIPS = 64
GLOCAL = 32
DEV_TILES = 8
N_TM = 4
N_DET = 8


def draw_coupling(key, part):
    first_key, second_key = jax.random.split(jax.random.fold_in(key, 5))
    diagonal = jax.random.uniform(first_key, (MODES,), jnp.float32, 0.5, 1.5)
    spread = 0.3
    offdiag = jax.random.normal(second_key, (MODES, MODES), jnp.float32) * (spread / math.sqrt(MODES))
    offdiag = jnp.clip(offdiag, -0.4, 0.4)
    return offdiag + jnp.diag(diagonal)


def device_pick(device_key):
    order_key, pick_key, shuffle_key = jax.random.split(device_key, 3)
    block_order = jax.random.permutation(order_key, N_DET)
    block_rank = jnp.argsort(block_order)
    pattern = jnp.where(jnp.arange(N_DET) % 2 == 0, CAPD, 2 * TOUCH - CAPD)
    counts = pattern[block_rank]
    block_shuffle = jax.vmap(lambda sub_key: jax.random.permutation(sub_key, GSHARE))(jax.random.split(pick_key, N_DET))
    chosen = block_shuffle[:, :CAPD]
    candidates = jnp.arange(N_DET, dtype=jnp.int32)[:, None] * GSHARE + chosen
    usable = jnp.arange(CAPD)[None, :] < counts[:, None]
    positions = jnp.arange(N_DET * CAPD, dtype=jnp.int32).reshape(N_DET, CAPD)
    sort_keys = jnp.where(usable, positions, positions + N_DET * CAPD).reshape(-1)
    picked = candidates.reshape(-1)[jnp.argsort(sort_keys)[:TOUCH * N_DET]]
    return picked[jax.random.permutation(shuffle_key, TOUCH * N_DET)]


def draw_device_slots(key, part):
    device_keys = jax.random.split(jax.random.fold_in(key, 11), N_TM * N_DET)
    picks = jax.vmap(device_pick)(device_keys)
    return picks.reshape(N_TM, N_DET * TOUCH * N_DET).astype(jnp.int32)


def block_homes(block_key):
    owner_key, place_key, shuffle_key = jax.random.split(block_key, 3)
    owners = jax.random.permutation(owner_key, N_TM)
    ranks_in = jnp.arange(GSHARE, dtype=jnp.int32)
    extra = jnp.maximum(ranks_in - CAPT, 0)
    owner_pos = jnp.where(ranks_in < CAPT, 0, 1 + extra % (N_TM - 1))
    place_rank = jnp.where(ranks_in < CAPT, ranks_in, extra // (N_TM - 1))
    places = jax.vmap(lambda sub_key: jax.random.permutation(sub_key, OWN))(jax.random.split(place_key, N_TM))
    owner_tm = owners[owner_pos]
    home_code = owner_tm * OWN + places[owner_tm, place_rank]
    return home_code[jax.random.permutation(shuffle_key, GSHARE)]


def draw_slot_home(key, part):
    block_keys = jax.random.split(jax.random.fold_in(key, 23), N_TM * N_DET)
    homes = jax.vmap(block_homes)(block_keys)
    return homes.reshape(N_TM, N_DET * GSHARE).astype(jnp.int32)


def plant(values, own_key, low, high):
    dims = values.shape
    place = [jax.random.randint(jax.random.fold_in(own_key, axis), (), 0, dims[axis]) for axis in range(len(dims))]
    values = values.at[tuple(place)].set(low)
    longest = dims.index(max(dims))
    place[longest] = (place[longest] + 1) % dims[longest]
    return values.at[tuple(place)].set(high)


def block_scale(stream_key, shape, cuts, low, largest):
    factor_of = 1.0
    for axis_at, parts in cuts:
        heights = jax.random.uniform(jax.random.fold_in(jax.random.fold_in(stream_key, 6), axis_at), (parts,), jnp.float32, low / len(cuts), largest / len(cuts))
        factor_of = factor_of * jnp.repeat(jnp.exp(heights), shape[axis_at] // parts).reshape((-1,) + (1,) * (len(shape) - 1 - axis_at))
    return factor_of


def noise(key, extent, scale, most, cuts=(), kind=jnp.bfloat16):
    array = jax.random.normal(key, extent, jnp.float32) * scale
    if len(cuts) > 0:
        array = block_scale(key, extent, cuts, -0.22, 0.18) * array
    return jnp.clip(array, min=-most, max=most).astype(kind)


def setup_inputs(seed: int = 0) -> dict:
    arg_keys = jax.random.split(jax.random.key(seed), 13)
    timestream = noise(arg_keys[0], (N_TM, DETS, SCANS * SAMPLES), 0.1, 0.8, ((0, 4), (1, 8)), jnp.float32)
    polar_angle = jnp.clip(jax.random.uniform(arg_keys[1], (N_TM, DETS, SCANS * SAMPLES), jnp.float32, -3.140625, 3.140625), -3.140625, 3.140625)
    pixel_index = plant(jax.random.randint(arg_keys[2], (N_TM, DETS, SCANS * SAMPLES), 0, TILE_PIX), jax.random.fold_in(arg_keys[2], 1), 0, TILE_PIX - 1).astype(jnp.int32)
    strip_tile = plant(jax.random.randint(arg_keys[3], (N_TM, DETS, STRIPS), 0, TOUCH * N_DET), jax.random.fold_in(arg_keys[3], 1), 0, (TOUCH * N_DET) - 1).astype(jnp.int32)
    time_const = jnp.clip(jnp.exp(math.log(2.0) - 2.3025851 * jax.random.uniform(arg_keys[4], (N_TM, DETS), jnp.float32) ** block_scale(arg_keys[4], (N_TM, DETS), ((0, 4), (1, 8)), -0.2, 0.2)), 0.2, 2.0)
    knee_freq = jnp.clip(jnp.exp(math.log(0.05) - 2.3025851 * jax.random.uniform(arg_keys[5], (N_TM, DETS), jnp.float32) ** block_scale(arg_keys[5], (N_TM, DETS), ((0, 4), (1, 8)), -0.2, 0.2)), 0.005, 0.05)
    noise_slope = jnp.clip(1.0 + 2.0 * jax.random.uniform(arg_keys[6], (N_TM, DETS), jnp.float32) ** block_scale(arg_keys[6], (N_TM, DETS), ((0, 4), (1, 8)), -0.2, 0.2), 1.0, 3.0)
    white_weight = jnp.clip(jnp.exp(math.log(2.0) - 1.3862944 * jax.random.uniform(arg_keys[7], (N_TM, DETS), jnp.float32) ** block_scale(arg_keys[7], (N_TM, DETS), ((0, 4), (1, 8)), -0.2, 0.2)), 0.5, 2.0)
    mode_mix = noise(arg_keys[8], (N_TM, DETS, MODES), (DETS // 4) ** -0.5, 1.0, ((0, 4), (1, 8)), jnp.float32)
    coupling = draw_coupling(jax.random.fold_in(arg_keys[12], 71), 0)
    device_slots = draw_device_slots(jax.random.fold_in(arg_keys[12], 71), 0)
    slot_home = draw_slot_home(jax.random.fold_in(arg_keys[12], 71), 0)
    return {"timestream": timestream, "polar_angle": polar_angle, "pixel_index": pixel_index, "strip_tile": strip_tile, "time_const": time_const, "knee_freq": knee_freq, "noise_slope": noise_slope, "white_weight": white_weight, "mode_mix": mode_mix, "coupling": coupling, "device_slots": device_slots, "slot_home": slot_home}


HIGHEST = lax.Precision.HIGHEST


def frequency_axis():
    positions = jnp.arange(SAMPLES, dtype=jnp.int32)
    return ((positions + SAMPLES // 2) % SAMPLES - SAMPLES // 2).astype(jnp.float32) / SAMPLES


def filtered(stream, time_const, knee_freq, noise_slope, white_weight, mode_mix, coupling):
    spectrum = jnp.fft.fft(stream, axis=-1)
    real_part = jnp.real(spectrum)
    imag_part = jnp.imag(spectrum)
    frequency = frequency_axis()
    power_law = jnp.power(jnp.abs(frequency)[None, :], noise_slope[:, None])
    weight = white_weight[:, None] * power_law / (power_law + jnp.power(knee_freq[:, None], noise_slope[:, None]))
    lag_phase = 2.0 * math.pi * frequency[None, :] * time_const[:, None]
    weighted_real = weight * (real_part - lag_phase * imag_part)
    weighted_imag = weight * (imag_part + lag_phase * real_part)
    stacked = jnp.concatenate([weighted_real, weighted_imag], axis=1)
    amplitudes = jnp.dot(mode_mix.T, stacked, precision=HIGHEST, preferred_element_type=jnp.float32)
    coupled = jnp.dot(coupling, amplitudes, precision=HIGHEST, preferred_element_type=jnp.float32)
    projected = jnp.dot(mode_mix, coupled, precision=HIGHEST, preferred_element_type=jnp.float32)
    weight_pair = jnp.concatenate([weight, weight], axis=1)
    cleaned = stacked - weight_pair * projected
    complexed = cleaned[:, :SAMPLES] + 1j * cleaned[:, SAMPLES:]
    return jnp.real(jnp.fft.ifft(complexed, axis=-1))


def group_partials(stream, polar_angle, pixel_index, strip_tile, slot_list):
    slot_table = slot_list.reshape(N_DET, DEV_TILES)
    owner_device = jnp.arange(DETS, dtype=jnp.int32) // DET_DEV
    strip_group = slot_table[owner_device[:, None], strip_tile]
    sample_slot = jnp.repeat(strip_group, STRIP, axis=1)
    flat_index = (sample_slot * (3 * TILE_PIX) + pixel_index).reshape(-1)
    values = stream.reshape(-1)
    twice = 2.0 * polar_angle.reshape(-1)
    segment_ids = jnp.concatenate([flat_index, flat_index + TILE_PIX, flat_index + 2 * TILE_PIX])
    payload = jnp.concatenate([values, values * jnp.cos(twice), values * jnp.sin(twice)])
    sums = jax.ops.segment_sum(payload, segment_ids, num_segments=GLOCAL * 3 * TILE_PIX)
    return sums.reshape(GLOCAL, 3, TILE_PIX)


def reference(timestream, polar_angle, pixel_index, strip_tile, time_const, knee_freq, noise_slope, white_weight, mode_mix, coupling, device_slots, slot_home):
    sky_map = jnp.zeros((N_TM * N_DET * OWN, 3, TILE_PIX), jnp.float32)
    slot_counter = jnp.arange(GLOCAL, dtype=jnp.int32)
    for group_index in range(N_TM):
        pieces = []
        for scan_index in range(SCANS):
            segment = timestream[group_index, :, scan_index * SAMPLES:(scan_index + 1) * SAMPLES]
            pieces.append(filtered(segment, time_const[group_index], knee_freq[group_index], noise_slope[group_index], white_weight[group_index], mode_mix[group_index], coupling))
        cleaned = jnp.concatenate(pieces, axis=1)
        partials = group_partials(cleaned, polar_angle[group_index], pixel_index[group_index], strip_tile[group_index], device_slots[group_index])
        home_code = slot_home[group_index]
        target_rows = ((home_code // OWN) * N_DET + slot_counter // GSHARE) * OWN + home_code % OWN
        sky_map = sky_map + jax.ops.segment_sum(partials, target_rows, num_segments=N_TM * N_DET * OWN)
    return sky_map
```

```python
import functools
import math

import jax
import jax.numpy as jnp
import numpy as np
from jax import lax
from jax.experimental import pallas as pl
from jax.experimental.pallas import tpu as pltpu
from jax.sharding import PartitionSpec as P

SAMPLES = 4096
TILE_PIX = 2048
CAPD = 2
CAPT = 2
OWN = 8
LANES = 128
OUTER = SAMPLES // LANES
HALF = OUTER // 2
TILE_ROWS = 3 * TILE_PIX // LANES
PIX_ROWS = TILE_PIX // LANES
SLOT_ROWS = TILE_ROWS + 8

HIGHEST = lax.Precision.HIGHEST
VMEM_LIMIT = 56 * 1024 * 1024


def transform_tables():
    b = np.arange(LANES)[:, None]
    q = np.arange(LANES)[None, :]
    cos = np.cos(2 * np.pi * (b * q % LANES) / LANES)
    sin = np.sin(2 * np.pi * (b * q % LANES) / LANES)
    forward = np.block([[cos, -sin], [sin, cos]])
    backward = np.block([[cos, sin], [-sin, cos]]) / SAMPLES
    h = LANES // 2
    even_f = np.concatenate([cos[:, :h], -sin[:, :h]], axis=1)
    even_f[:, h] = cos[:, h]
    even_b = np.concatenate([2 * cos[:h], -2 * sin[:h]], axis=0)
    even_b[0] = 1.0
    even_b[h] = cos[h]
    odd_phase = 2 * np.pi * (b * (2 * np.arange(h)[None, :] + 1) % (2 * LANES)) / (2 * LANES)
    odd_f = np.concatenate([np.cos(odd_phase), -np.sin(odd_phase)], axis=1)
    odd_b = np.concatenate([2 * np.cos(odd_phase).T, -2 * np.sin(odd_phase).T], axis=0)
    zero = np.zeros((LANES, LANES))
    packed_f = np.block([[even_f, zero], [zero, odd_f]])
    packed_b = np.block([[even_b, zero], [zero, odd_b]]) / SAMPLES
    matrices = np.stack([packed_f, forward, packed_b, backward]).astype(np.float32)
    k1 = np.arange(HALF)[:, None]
    angle = 2 * np.pi * (k1 * q) / SAMPLES
    k = k1 + OUTER * q
    freq = (((k + SAMPLES // 2) % SAMPLES) - SAMPLES // 2) / SAMPLES
    lane = np.arange(LANES)
    low = lane % h
    even_k = OUTER * low
    even_k[h] = SAMPLES // 2
    odd_k = HALF + OUTER * low
    even_freq = (((even_k + SAMPLES // 2) % SAMPLES) - SAMPLES // 2) / SAMPLES
    odd_freq = (((odd_k + SAMPLES // 2) % SAMPLES) - SAMPLES // 2) / SAMPLES
    freq = np.concatenate([freq, odd_freq[None]], axis=0)
    freq[0] = even_freq
    with np.errstate(divide="ignore"):
        logs = np.where(freq == 0.0, -1e30, np.log2(np.abs(freq)))
    lag = 2 * np.pi * freq
    even_lag = np.where(lane < h, -lag[0], lag[0])
    even_lag[h] = 0.0
    even_lag[0] = 0.0
    odd_lag = np.where(lane < h, -lag[HALF], lag[HALF])
    lag[0] = even_lag
    lag[HALF] = odd_lag
    twist = np.stack([np.cos(angle), np.sin(angle)])
    rows = np.concatenate([twist[0], twist[1], logs, lag], axis=0)
    rows = np.concatenate([rows, np.zeros((-rows.shape[0] % 8, LANES))], axis=0)
    return matrices, rows.astype(np.float32)


ROW_COS, ROW_SIN, ROW_LOG, ROW_LAG = 0, HALF, 2 * HALF, 3 * HALF + 1


def add(x, y):
    return y if x is None else (x if y is None else x + y)


def sub(x, y):
    if y is None:
        return x
    return -y if x is None else x - y


def rotate(re, im, c, s):
    if abs(s) < 1e-12:
        return (re, im) if c > 0 else (-re, None if im is None else -im)
    if abs(c) < 1e-12:
        flip = None if im is None else (-im if s > 0 else im)
        return flip, (re if s > 0 else -re)
    if im is None:
        return re * c, re * s
    return re * c - im * s, im * c + re * s


def real_forward(xs):
    n = len(xs)
    if n == 1:
        return [xs[0]], [None]
    if n == 2:
        return [xs[0] + xs[1], xs[0] - xs[1]], [None, None]
    er, ei = real_forward(xs[0::2])
    odr, odi = real_forward(xs[1::2])
    re, im = [None] * (n // 2 + 1), [None] * (n // 2 + 1)
    for k in range(n // 4 + 1):
        angle = -2.0 * math.pi * k / n
        pr, pi_ = rotate(odr[k], odi[k], math.cos(angle), math.sin(angle))
        re[k], im[k] = add(er[k], pr), add(ei[k], pi_)
        if k < n // 4:
            re[n // 2 - k] = sub(er[k], pr)
            tail = sub(ei[k], pi_)
            im[n // 2 - k] = None if tail is None else -tail
    return re, im


def real_backward(re, im):
    n = 2 * (len(re) - 1)
    if n == 2:
        return [re[0] + re[1], re[0] - re[1]]
    er, ei, odr, odi = [], [], [], []
    for k in range(n // 4 + 1):
        m = n // 2 - k
        if k == 0:
            er.append(re[0] + re[m])
            ei.append(None)
            odr.append(re[0] - re[m])
            odi.append(None)
        elif k == m:
            er.append(2.0 * re[k])
            ei.append(None)
            odr.append(-2.0 * im[k])
            odi.append(None)
        else:
            er.append(re[k] + re[m])
            ei.append(im[k] - im[m])
            angle = 2.0 * math.pi * k / n
            pr, pi_ = rotate(re[k] - re[m], im[k] + im[m], math.cos(angle), math.sin(angle))
            odr.append(pr)
            odi.append(pi_)
    even, odd = real_backward(er, ei), real_backward(odr, odi)
    return [v for pair in zip(even, odd) for v in pair]


def split_bf16(x):
    high = x.astype(jnp.bfloat16)
    return high, (x - high.astype(jnp.float32)).astype(jnp.bfloat16)


def dot32(x, y):
    return jnp.dot(x, y, precision=HIGHEST, preferred_element_type=jnp.float32)


def column(row_ref, dets):
    wide = jnp.broadcast_to(row_ref[...], (dets, dets))
    own = lax.broadcasted_iota(jnp.int32, (dets, dets), 0) == lax.broadcasted_iota(jnp.int32, (dets, dets), 1)
    return jnp.sum(jnp.where(own, wide, 0.0), axis=1, keepdims=True)


def table_row(rows_ref, row, shape):
    return jnp.broadcast_to(rows_ref[row : row + 1, :], shape)


def spectra(ts_ref, tc_ref, knee_ref, slope_ref, white_ref, mat_ref, rows_ref, work_ref, w_ref, nw_ref):
    dets = ts_ref.shape[1]
    scans = ts_ref.shape[2] // SAMPLES
    for scan in range(scans):
        for d0 in range(0, dets, 8):
            xs = [ts_ref[0, d0 : d0 + 8, (scan * OUTER + a) * LANES : (scan * OUTER + a + 1) * LANES] for a in range(OUTER)]
            re, im = real_forward(xs)
            for k1 in range(HALF):
                r = (k1 * scans + scan) * dets + d0
                if k1 == 0:
                    out_re, out_im = re[0], re[HALF]
                else:
                    c = table_row(rows_ref, ROW_COS + k1, (8, LANES))
                    s = table_row(rows_ref, ROW_SIN + k1, (8, LANES))
                    out_re, out_im = re[k1] * c + im[k1] * s, im[k1] * c - re[k1] * s
                work_ref[r : r + 8, :LANES] = out_re
                work_ref[r : r + 8, LANES:] = out_im
    head = scans * dets
    work_ref[:head, :] = dot32(work_ref[:head, :], mat_ref[0])
    work_ref[head:, :] = dot32(work_ref[head:, :], mat_ref[1])
    slope, knee, tau = column(slope_ref, dets), column(knee_ref, dets), column(tc_ref, dets)
    white = column(white_ref, dets)
    knee_pow = jnp.exp2(slope * jnp.log2(knee))
    shape = (dets, LANES)
    slope, knee_pow = jnp.broadcast_to(slope, shape), jnp.broadcast_to(knee_pow, shape)
    tau, white = jnp.broadcast_to(tau, shape), jnp.broadcast_to(white, shape)
    for row in range(HALF + 1):
        power = jnp.exp2(slope * table_row(rows_ref, ROW_LOG + row, shape))
        weight = white * power / (power + knee_pow)
        nw_ref[row] = weight
        lag = tau * table_row(rows_ref, ROW_LAG + row, shape)
        for scan in range(scans):
            if row == 0 or row == HALF:
                r = scan * dets
                part = 0 if row == 0 else 1
                v = work_ref[r : r + dets, part * LANES : (part + 1) * LANES]
                w_ref[part * HALF * scans + scan] = weight * (v + lag * pltpu.roll(v, LANES // 2, 1))
            else:
                r = (row * scans + scan) * dets
                re, im = work_ref[r : r + dets, :LANES], work_ref[r : r + dets, LANES:]
                w_ref[row * scans + scan] = weight * (re - lag * im)
                w_ref[(HALF + row) * scans + scan] = weight * (im + lag * re)


def streams(w_ref, p_ref, nw_ref, mat_ref, rows_ref, work_ref, store):
    dets = w_ref.shape[1]
    scans = w_ref.shape[0] // (2 * HALF)
    for part in range(2):
        for k1 in range(HALF):
            row = HALF if (part == 1 and k1 == 0) else k1
            for scan in range(scans):
                i = (part * HALF + k1) * scans + scan
                r = (k1 * scans + scan) * dets
                work_ref[r : r + dets, part * LANES : (part + 1) * LANES] = w_ref[i] - nw_ref[row] * p_ref[i]
    head = scans * dets
    work_ref[:head, :] = dot32(work_ref[:head, :], mat_ref[2])
    work_ref[head:, :] = dot32(work_ref[head:, :], mat_ref[3])
    for scan in range(scans):
        for d0 in range(0, dets, 8):
            re, im = [], []
            for k1 in range(HALF):
                r = (k1 * scans + scan) * dets + d0
                zr, zi = work_ref[r : r + 8, :LANES], work_ref[r : r + 8, LANES:]
                if k1 == 0:
                    re.append(zr)
                    im.append(None)
                    last = zi
                else:
                    c = table_row(rows_ref, ROW_COS + k1, (8, LANES))
                    s = table_row(rows_ref, ROW_SIN + k1, (8, LANES))
                    re.append(zr * c - zi * s)
                    im.append(zi * c + zr * s)
            re.append(last)
            im.append(None)
            for a, value in enumerate(real_backward(re, im)):
                store(scan, d0, a, value)


def forward_kernel(n_det, ts_ref, tc_ref, knee_ref, slope_ref, white_ref, mix_ref, mat_ref, rows_ref,
                   send_ref, w_ref, nw_ref, work_ref):
    spectra(ts_ref, tc_ref, knee_ref, slope_ref, white_ref, mat_ref, rows_ref, work_ref, w_ref, nw_ref)
    share = w_ref.shape[0] // n_det
    modes = mix_ref.shape[2]
    for j in range(n_det):
        for r in range(share):
            send_ref[j, r] = w_ref[j * share + r]
        send_ref[j, share, :, :modes] = mix_ref[0]
        send_ref[j, share, :, modes:] = jnp.zeros((mix_ref.shape[1], LANES - modes), jnp.float32)


def couple_kernel(n_det, got_ref, cpl_ref, out_ref):
    share = got_ref.shape[1] - 1
    dets = got_ref.shape[2]
    modes = cpl_ref.shape[0]
    mix = jnp.concatenate([got_ref[j, share] for j in range(n_det)], axis=0)[:, :modes]
    shift = dot32(mix, cpl_ref[...])
    gram = lax.dot_general(shift, mix, (((1,), (1,)), ((), ())), precision=HIGHEST,
                           preferred_element_type=jnp.float32)
    for r in range(share):
        block = jnp.concatenate([got_ref[j, r] for j in range(n_det)], axis=0)
        back = dot32(gram, block)
        for j in range(n_det):
            out_ref[j, r] = back[j * dets : (j + 1) * dets]


def backward_kernel(w_ref, p_ref, nw_ref, mat_ref, rows_ref, out_ref, work_ref):
    def store(scan, d0, a, value):
        s = scan * OUTER + a
        out_ref[s, d0 : d0 + 8, :] = value

    streams(w_ref, p_ref, nw_ref, mat_ref, rows_ref, work_ref, store)


def turn_polynomials():
    x = (np.cos(np.pi * (np.arange(400) + 0.5) / 400) + 1) / 8
    t = np.sqrt(x)
    cheb = np.polynomial.Polynomial
    cos_fit = cheb.fit(x, np.cos(2 * np.pi * t), 7).convert().coef
    sin_fit = cheb.fit(x, np.sin(2 * np.pi * t) / t, 7).convert().coef
    return [float(np.float32(c)) for c in cos_fit], [float(np.float32(c)) for c in sin_fit]


COS_FIT, SIN_FIT = turn_polynomials()


def horner(coefficients, x):
    total = jnp.full_like(x, coefficients[-1])
    for c in coefficients[-2::-1]:
        total = total * x + c
    return total


def bin_kernel(gshare, stream_ref, angle_ref, pix_ref, tile_ref, slots_ref, out_ref, target_ref, count_ref):
    strips, dets, _ = stream_ref.shape
    n_slots = slots_ref.shape[1]
    peers = out_ref.shape[0] // CAPD

    def clear(i, carry):
        out_ref[i, :TILE_ROWS, :] = jnp.zeros((TILE_ROWS, LANES), jnp.float32)
        out_ref[i, TILE_ROWS:, :] = jnp.full((8, LANES), -1.0, jnp.float32)
        return carry

    lax.fori_loop(0, peers * CAPD, clear, 0)

    def reset(i, carry):
        count_ref[i] = 0
        return carry

    lax.fori_loop(0, peers, reset, 0)

    def place(i, carry):
        entry = slots_ref[0, i]
        peer = entry // gshare
        rank = count_ref[peer]
        count_ref[peer] = rank + 1
        target = peer * CAPD + rank
        target_ref[i] = target
        out_ref[target, TILE_ROWS:, :] = jnp.full((8, LANES), (entry - peer * gshare).astype(jnp.float32))
        return carry

    lax.fori_loop(0, n_slots, place, 0)

    low_iota = lax.broadcasted_iota(jnp.int32, (LANES, LANES), 0).astype(jnp.float32).astype(jnp.bfloat16)
    high_iota = lax.broadcasted_iota(jnp.int32, (PIX_ROWS, LANES), 0).astype(jnp.float32).astype(jnp.bfloat16)
    one, zero = jnp.bfloat16(1.0), jnp.bfloat16(0.0)

    def strip(s, carry):
        lanes = pl.ds(pl.multiple_of(s * LANES, LANES), LANES)
        value = stream_ref[s]
        turn = angle_ref[0, :, lanes] * (1.0 / math.pi)
        turn = turn - jnp.round(turn)
        square = turn * turn
        parts = [value, value * horner(COS_FIT, square), value * turn * horner(SIN_FIT, square)]
        halves = [split_bf16(v) for v in parts]
        halves = [h[0] for h in halves] + [h[1] for h in halves]
        pix = pix_ref[0, :, lanes]
        high = (pix >> 7).astype(jnp.float32).astype(jnp.bfloat16)
        low = (pix & (LANES - 1)).astype(jnp.float32).astype(jnp.bfloat16)
        for d in range(dets):
            hit = high_iota == high[d : d + 1, :]
            rows = jnp.concatenate([jnp.where(hit, h[d : d + 1, :], zero) for h in halves], axis=0)
            spread = jnp.where(low_iota == low[d : d + 1, :], one, zero)
            both = lax.dot_general(rows, spread, (((1,), (1,)), ((), ())), preferred_element_type=jnp.float32)
            target = target_ref[tile_ref[0, d, s]]
            out_ref[target, :TILE_ROWS, :] += both[:TILE_ROWS] + both[TILE_ROWS:]
        return carry

    lax.fori_loop(0, strips, strip, 0)


def regroup_kernel(got_ref, home_ref, out_ref, block_ref, count_ref):
    gshare = home_ref.shape[1]
    received = got_ref.shape[0]
    peers = out_ref.shape[0] // CAPT
    block_ref[...] = jnp.zeros_like(block_ref)

    def gather(i, carry):
        label = got_ref[i, TILE_ROWS : TILE_ROWS + 1, :]
        tile = got_ref[i, :TILE_ROWS, :]
        for e in range(gshare):
            block_ref[e] += jnp.where(label == float(e), tile, 0.0)
        return carry

    lax.fori_loop(0, received, gather, 0)
    out_ref[:, :TILE_ROWS, :] = jnp.zeros((peers * CAPT, TILE_ROWS, LANES), jnp.float32)
    out_ref[:, TILE_ROWS:, :] = jnp.full((peers * CAPT, 8, LANES), -1.0, jnp.float32)
    for p in range(peers):
        count_ref[p] = 0
    for e in range(gshare):
        code = home_ref[0, e]
        peer = code // OWN
        rank = count_ref[peer]
        count_ref[peer] = rank + 1
        target = peer * CAPT + rank
        out_ref[target, :TILE_ROWS, :] = block_ref[e]
        out_ref[target, TILE_ROWS:, :] = jnp.full((8, LANES), (code - peer * OWN).astype(jnp.float32))


def final_kernel(got_ref, out_ref):
    for t in range(OWN):
        for c in range(3):
            total = jnp.zeros((PIX_ROWS, LANES), jnp.float32)
            for i in range(got_ref.shape[0]):
                label = got_ref[i, TILE_ROWS : TILE_ROWS + 1, :]
                total = total + jnp.where(label == float(t), got_ref[i, c * PIX_ROWS : (c + 1) * PIX_ROWS, :], 0.0)
            out_ref[t, c] = total


def per_device(timestream, polar_angle, pixel_index, strip_tile, time_const, knee_freq, noise_slope,
               white_weight, mode_mix, coupling, device_slots, slot_home):
    dets, total = timestream.shape[1:]
    scans = total // SAMPLES
    n_det, n_tm = lax.axis_size("det"), lax.axis_size("tm")
    matrices, rows = transform_tables()
    matrices, rows = jnp.asarray(matrices), jnp.asarray(rows)
    blocks = 2 * HALF * scans
    share = blocks // n_det
    f32 = jnp.float32
    vmem = pl.BlockSpec(memory_space=pltpu.VMEM)
    smem = pl.BlockSpec(memory_space=pltpu.SMEM)
    params = pltpu.CompilerParams(vmem_limit_bytes=VMEM_LIMIT)
    work = pltpu.VMEM((HALF * scans * dets, 2 * LANES), f32)
    send, weighted, weight = pl.pallas_call(
        functools.partial(forward_kernel, n_det),
        out_shape=(
            jax.ShapeDtypeStruct((n_det, share + 1, dets, LANES), f32),
            jax.ShapeDtypeStruct((blocks, dets, LANES), f32),
            jax.ShapeDtypeStruct((HALF + 1, dets, LANES), f32),
        ),
        in_specs=[vmem] * 8,
        out_specs=(vmem,) * 3,
        scratch_shapes=[work],
        compiler_params=params,
        name="forward",
    )(timestream, time_const, knee_freq, noise_slope, white_weight, mode_mix, matrices, rows)
    got = lax.all_to_all(send, "det", split_axis=0, concat_axis=0, tiled=True)
    back = pl.pallas_call(
        functools.partial(couple_kernel, n_det),
        out_shape=jax.ShapeDtypeStruct((n_det, share, dets, LANES), f32),
        in_specs=[vmem] * 2,
        out_specs=vmem,
        compiler_params=params,
        name="couple",
    )(got, coupling)
    projected = lax.all_to_all(back, "det", split_axis=0, concat_axis=0, tiled=True).reshape(blocks, dets, LANES)
    stream = pl.pallas_call(
        backward_kernel,
        out_shape=jax.ShapeDtypeStruct((scans * OUTER, dets, LANES), f32),
        in_specs=[vmem] * 5,
        out_specs=vmem,
        scratch_shapes=[work],
        compiler_params=params,
        name="backward",
    )(weighted, projected, weight, matrices, rows)
    tiles = pl.pallas_call(
        functools.partial(bin_kernel, slot_home.shape[1]),
        out_shape=jax.ShapeDtypeStruct((n_det * CAPD, SLOT_ROWS, LANES), f32),
        in_specs=[vmem] * 3 + [smem] * 2,
        out_specs=vmem,
        scratch_shapes=[pltpu.SMEM((device_slots.shape[1],), jnp.int32), pltpu.SMEM((n_det,), jnp.int32)],
        compiler_params=params,
        name="binning",
    )(stream, polar_angle, pixel_index, strip_tile, device_slots)
    tiles = lax.all_to_all(tiles, "det", split_axis=0, concat_axis=0, tiled=True)
    homes = pl.pallas_call(
        regroup_kernel,
        out_shape=jax.ShapeDtypeStruct((n_tm * CAPT, SLOT_ROWS, LANES), f32),
        in_specs=[vmem, smem],
        out_specs=vmem,
        scratch_shapes=[pltpu.VMEM((slot_home.shape[1], TILE_ROWS, LANES), f32), pltpu.SMEM((n_tm,), jnp.int32)],
        compiler_params=params,
        name="regroup",
    )(tiles, slot_home)
    homes = lax.all_to_all(homes, "tm", split_axis=0, concat_axis=0, tiled=True)
    out = pl.pallas_call(
        final_kernel,
        out_shape=jax.ShapeDtypeStruct((OWN, 3, PIX_ROWS, LANES), f32),
        in_specs=[vmem],
        out_specs=vmem,
        compiler_params=params,
        name="place",
    )(homes)
    return out.reshape(OWN, 3, TILE_PIX)


def solution(mesh):
    placed = (
        P("tm", "det", None),
        P("tm", "det", None),
        P("tm", "det", None),
        P("tm", "det", None),
        P("tm", "det"),
        P("tm", "det"),
        P("tm", "det"),
        P("tm", "det"),
        P("tm", "det", None),
        P(),
        P("tm", "det"),
        P("tm", "det"),
    )
    return jax.shard_map(
        per_device,
        mesh=mesh,
        in_specs=placed,
        out_specs=P(("tm", "det"), None, None),
        check_vma=False,
    )
```

```python
import functools
import math

import jax
import jax.numpy as jnp
import numpy as np
from jax import lax
from jax.experimental import pallas as pl
from jax.experimental.pallas import tpu as pltpu
from jax.sharding import PartitionSpec as P

SAMPLES = 4096
TILE_PIX = 2048
CAPD = 2
CAPT = 2
OWN = 8
LANES = 128
OUTER = SAMPLES // LANES
HALF = OUTER // 2
TILE_ROWS = 3 * TILE_PIX // LANES
PIX_ROWS = TILE_PIX // LANES
SLOT_ROWS = TILE_ROWS + 8

HIGHEST = lax.Precision.HIGHEST
VMEM_LIMIT = 56 * 1024 * 1024


def transform_tables():
    b = np.arange(LANES)[:, None]
    q = np.arange(LANES)[None, :]
    cos = np.cos(2 * np.pi * (b * q % LANES) / LANES)
    sin = np.sin(2 * np.pi * (b * q % LANES) / LANES)
    forward = np.block([[cos, -sin], [sin, cos]])
    backward = np.block([[cos, sin], [-sin, cos]]) / SAMPLES
    h = LANES // 2
    even_f = np.concatenate([cos[:, :h], -sin[:, :h]], axis=1)
    even_f[:, h] = cos[:, h]
    even_b = np.concatenate([2 * cos[:h], -2 * sin[:h]], axis=0)
    even_b[0] = 1.0
    even_b[h] = cos[h]
    odd_phase = 2 * np.pi * (b * (2 * np.arange(h)[None, :] + 1) % (2 * LANES)) / (2 * LANES)
    odd_f = np.concatenate([np.cos(odd_phase), -np.sin(odd_phase)], axis=1)
    odd_b = np.concatenate([2 * np.cos(odd_phase).T, -2 * np.sin(odd_phase).T], axis=0)
    zero = np.zeros((LANES, LANES))
    packed_f = np.block([[even_f, zero], [zero, odd_f]])
    packed_b = np.block([[even_b, zero], [zero, odd_b]]) / SAMPLES
    matrices = np.stack([packed_f, forward, packed_b, backward]).astype(np.float32)
    k1 = np.arange(HALF)[:, None]
    angle = 2 * np.pi * (k1 * q) / SAMPLES
    k = k1 + OUTER * q
    freq = (((k + SAMPLES // 2) % SAMPLES) - SAMPLES // 2) / SAMPLES
    lane = np.arange(LANES)
    low = lane % h
    even_k = OUTER * low
    even_k[h] = SAMPLES // 2
    odd_k = HALF + OUTER * low
    even_freq = (((even_k + SAMPLES // 2) % SAMPLES) - SAMPLES // 2) / SAMPLES
    odd_freq = (((odd_k + SAMPLES // 2) % SAMPLES) - SAMPLES // 2) / SAMPLES
    freq = np.concatenate([freq, odd_freq[None]], axis=0)
    freq[0] = even_freq
    with np.errstate(divide="ignore"):
        logs = np.where(freq == 0.0, -1e30, np.log2(np.abs(freq)))
    lag = 2 * np.pi * freq
    even_lag = np.where(lane < h, -lag[0], lag[0])
    even_lag[h] = 0.0
    even_lag[0] = 0.0
    odd_lag = np.where(lane < h, -lag[HALF], lag[HALF])
    lag[0] = even_lag
    lag[HALF] = odd_lag
    twist = np.stack([np.cos(angle), np.sin(angle)])
    rows = np.concatenate([twist[0], twist[1], logs, lag], axis=0)
    rows = np.concatenate([rows, np.zeros((-rows.shape[0] % 8, LANES))], axis=0)
    return matrices, rows.astype(np.float32)


ROW_COS, ROW_SIN, ROW_LOG, ROW_LAG = 0, HALF, 2 * HALF, 3 * HALF + 1


def add(x, y):
    return y if x is None else (x if y is None else x + y)


def sub(x, y):
    if y is None:
        return x
    return -y if x is None else x - y


def rotate(re, im, c, s):
    if abs(s) < 1e-12:
        return (re, im) if c > 0 else (-re, None if im is None else -im)
    if abs(c) < 1e-12:
        flip = None if im is None else (-im if s > 0 else im)
        return flip, (re if s > 0 else -re)
    if im is None:
        return re * c, re * s
    return re * c - im * s, im * c + re * s


def real_forward(xs):
    n = len(xs)
    if n == 1:
        return [xs[0]], [None]
    if n == 2:
        return [xs[0] + xs[1], xs[0] - xs[1]], [None, None]
    er, ei = real_forward(xs[0::2])
    odr, odi = real_forward(xs[1::2])
    re, im = [None] * (n // 2 + 1), [None] * (n // 2 + 1)
    for k in range(n // 4 + 1):
        angle = -2.0 * math.pi * k / n
        pr, pi_ = rotate(odr[k], odi[k], math.cos(angle), math.sin(angle))
        re[k], im[k] = add(er[k], pr), add(ei[k], pi_)
        if k < n // 4:
            re[n // 2 - k] = sub(er[k], pr)
            tail = sub(ei[k], pi_)
            im[n // 2 - k] = None if tail is None else -tail
    return re, im


def real_backward(re, im):
    n = 2 * (len(re) - 1)
    if n == 2:
        return [re[0] + re[1], re[0] - re[1]]
    er, ei, odr, odi = [], [], [], []
    for k in range(n // 4 + 1):
        m = n // 2 - k
        if k == 0:
            er.append(re[0] + re[m])
            ei.append(None)
            odr.append(re[0] - re[m])
            odi.append(None)
        elif k == m:
            er.append(2.0 * re[k])
            ei.append(None)
            odr.append(-2.0 * im[k])
            odi.append(None)
        else:
            er.append(re[k] + re[m])
            ei.append(im[k] - im[m])
            angle = 2.0 * math.pi * k / n
            pr, pi_ = rotate(re[k] - re[m], im[k] + im[m], math.cos(angle), math.sin(angle))
            odr.append(pr)
            odi.append(pi_)
    even, odd = real_backward(er, ei), real_backward(odr, odi)
    return [v for pair in zip(even, odd) for v in pair]


def split_bf16(x):
    high = x.astype(jnp.bfloat16)
    return high, (x - high.astype(jnp.float32)).astype(jnp.bfloat16)


def dot32(x, y):
    return jnp.dot(x, y, precision=HIGHEST, preferred_element_type=jnp.float32)


def column(row_ref, dets):
    wide = jnp.broadcast_to(row_ref[...], (dets, dets))
    own = lax.broadcasted_iota(jnp.int32, (dets, dets), 0) == lax.broadcasted_iota(jnp.int32, (dets, dets), 1)
    return jnp.sum(jnp.where(own, wide, 0.0), axis=1, keepdims=True)


def table_row(rows_ref, row, shape):
    return jnp.broadcast_to(rows_ref[row : row + 1, :], shape)


def noise_weights(tc_ref, knee_ref, slope_ref, white_ref, rows_ref, nw_ref, lag_ref):
    dets = tc_ref.shape[1]
    shape = (dets, LANES)
    slope, knee = column(slope_ref, dets), column(knee_ref, dets)
    knee_pow = jnp.broadcast_to(jnp.exp2(slope * jnp.log2(knee)), shape)
    slope = jnp.broadcast_to(slope, shape)
    tau, white = jnp.broadcast_to(column(tc_ref, dets), shape), jnp.broadcast_to(column(white_ref, dets), shape)
    for row in range(HALF + 1):
        power = jnp.exp2(slope * table_row(rows_ref, ROW_LOG + row, shape))
        nw_ref[row] = white * power / (power + knee_pow)
        lag_ref[row] = tau * table_row(rows_ref, ROW_LAG + row, shape)


def spectra(scan, ts_ref, mat_ref, rows_ref, nw_ref, lag_ref, work_ref, w_ref):
    dets = ts_ref.shape[1]
    for d0 in range(0, dets, 8):
        xs = [ts_ref[0, d0 : d0 + 8, (scan * OUTER + a) * LANES : (scan * OUTER + a + 1) * LANES] for a in range(OUTER)]
        re, im = real_forward(xs)
        for k1 in range(HALF):
            r = k1 * dets + d0
            if k1 == 0:
                out_re, out_im = re[0], re[HALF]
            else:
                c = table_row(rows_ref, ROW_COS + k1, (8, LANES))
                s = table_row(rows_ref, ROW_SIN + k1, (8, LANES))
                out_re, out_im = re[k1] * c + im[k1] * s, im[k1] * c - re[k1] * s
            work_ref[r : r + 8, :LANES] = out_re
            work_ref[r : r + 8, LANES:] = out_im
    work_ref[:dets, :] = dot32(work_ref[:dets, :], mat_ref[0])
    work_ref[dets:, :] = dot32(work_ref[dets:, :], mat_ref[1])
    for k1 in range(HALF):
        r = k1 * dets
        re, im = work_ref[r : r + dets, :LANES], work_ref[r : r + dets, LANES:]
        if k1 == 0:
            w_ref[scan, 0] = nw_ref[0] * (re + lag_ref[0] * pltpu.roll(re, LANES // 2, 1))
            w_ref[scan, HALF] = nw_ref[HALF] * (im + lag_ref[HALF] * pltpu.roll(im, LANES // 2, 1))
        else:
            w_ref[scan, k1] = nw_ref[k1] * (re - lag_ref[k1] * im)
            w_ref[scan, HALF + k1] = nw_ref[k1] * (im + lag_ref[k1] * re)


def streams(scan, w_ref, p_ref, nw_ref, mat_ref, rows_ref, work_ref, out_ref):
    dets = w_ref.shape[2]
    for part in range(2):
        for k1 in range(HALF):
            row = HALF if (part == 1 and k1 == 0) else k1
            i = part * HALF + k1
            r = k1 * dets
            work_ref[r : r + dets, part * LANES : (part + 1) * LANES] = w_ref[scan, i] - nw_ref[row] * p_ref[scan, i]
    work_ref[:dets, :] = dot32(work_ref[:dets, :], mat_ref[2])
    work_ref[dets:, :] = dot32(work_ref[dets:, :], mat_ref[3])
    for d0 in range(0, dets, 8):
        re, im = [], []
        for k1 in range(HALF):
            r = k1 * dets + d0
            zr, zi = work_ref[r : r + 8, :LANES], work_ref[r : r + 8, LANES:]
            if k1 == 0:
                re.append(zr)
                im.append(None)
                last = zi
            else:
                c = table_row(rows_ref, ROW_COS + k1, (8, LANES))
                s = table_row(rows_ref, ROW_SIN + k1, (8, LANES))
                re.append(zr * c - zi * s)
                im.append(zi * c + zr * s)
        re.append(last)
        im.append(None)
        for a, value in enumerate(real_backward(re, im)):
            out_ref[scan * OUTER + a, d0 : d0 + 8, :] = value


def remote(src, dst, send_sem, recv_sem, device):
    return pltpu.make_async_remote_copy(
        src_ref=src, dst_ref=dst, send_sem=send_sem, recv_sem=recv_sem, device_id=device,
        device_id_type=pl.DeviceIdType.MESH,
    )


def clean_kernel(n, ts_ref, tc_ref, knee_ref, slope_ref, white_ref, mix_ref, cpl_ref, mat_ref, rows_ref, out_ref,
                 w_ref, p_ref, nw_ref, lag_ref, work_ref, mine_ref, mix_all_ref, got_ref, back_ref,
                 mix_sems, out_sems, back_sems):
    me = lax.axis_index("det")
    scans, rows_all, dets, _ = w_ref.shape
    share = rows_all // n
    modes = mix_ref.shape[2]
    offsets = range(1, n)
    ahead = [lax.rem(me + o, n) for o in range(n)]
    behind = [lax.rem(me + n - o, n) for o in range(n)]
    barrier = pltpu.get_barrier_semaphore()
    for o in offsets:
        pl.semaphore_signal(barrier, inc=1, device_id={"det": ahead[o]}, device_id_type=pl.DeviceIdType.MESH)
    pl.semaphore_wait(barrier, n - 1)
    mine = jnp.concatenate([mix_ref[0], jnp.zeros((dets, LANES - modes), jnp.float32)], axis=1)
    mine_ref[...] = mine
    mix_all_ref[0] = mine
    copies = []
    for o in offsets:
        copy = remote(mine_ref, mix_all_ref.at[o], mix_sems.at[0, o], mix_sems.at[1, o], {"det": ahead[o]})
        copy.start()
        copies.append(copy)
    noise_weights(tc_ref, knee_ref, slope_ref, white_ref, rows_ref, nw_ref, lag_ref)
    outgoing = []
    for scan in range(scans):
        spectra(scan, ts_ref, mat_ref, rows_ref, nw_ref, lag_ref, work_ref, w_ref)
        sent = []
        for o in offsets:
            copy = remote(w_ref.at[scan, pl.ds(ahead[o] * share, share)], got_ref.at[scan, o],
                          out_sems.at[0, scan, o], out_sems.at[1, scan, o], {"det": ahead[o]})
            copy.start()
            sent.append(copy)
        outgoing.append(sent)
        got_ref[scan, 0] = w_ref[scan, pl.ds(me * share, share)]
    for copy in copies:
        copy.wait()
    mix = jnp.concatenate([mix_all_ref[o] for o in range(n)], axis=0)[:, :modes]
    gram = lax.dot_general(dot32(mix, cpl_ref[...]), mix, (((1,), (1,)), ((), ())), precision=HIGHEST,
                           preferred_element_type=jnp.float32)
    returning = []
    for scan in range(scans):
        for copy in outgoing[scan]:
            copy.wait()
        for r in range(share):
            block = jnp.concatenate([got_ref[scan, o, r] for o in range(n)], axis=0)
            back = dot32(gram, block)
            for o in range(n):
                back_ref[scan, o, r] = back[o * dets : (o + 1) * dets]
        sent = []
        for o in offsets:
            copy = remote(back_ref.at[scan, o], p_ref.at[scan, pl.ds(me * share, share)],
                          back_sems.at[0, scan, o], back_sems.at[1, scan, o], {"det": behind[o]})
            copy.start()
            sent.append(copy)
        returning.append(sent)
        p_ref[scan, pl.ds(me * share, share)] = back_ref[scan, 0]
    for scan in range(scans):
        for copy in returning[scan]:
            copy.wait()
        streams(scan, w_ref, p_ref, nw_ref, mat_ref, rows_ref, work_ref, out_ref)


def turn_polynomials():
    x = (np.cos(np.pi * (np.arange(400) + 0.5) / 400) + 1) / 8
    t = np.sqrt(x)
    cheb = np.polynomial.Polynomial
    cos_fit = cheb.fit(x, np.cos(2 * np.pi * t), 7).convert().coef
    sin_fit = cheb.fit(x, np.sin(2 * np.pi * t) / t, 7).convert().coef
    return [float(np.float32(c)) for c in cos_fit], [float(np.float32(c)) for c in sin_fit]


COS_FIT, SIN_FIT = turn_polynomials()


def horner(coefficients, x):
    total = jnp.full_like(x, coefficients[-1])
    for c in coefficients[-2::-1]:
        total = total * x + c
    return total


def bin_kernel(gshare, stream_ref, angle_ref, pix_ref, tile_ref, slots_ref, out_ref, target_ref, count_ref):
    strips, dets, _ = stream_ref.shape
    n_slots = slots_ref.shape[1]
    peers = out_ref.shape[0] // CAPD

    def clear(i, carry):
        out_ref[i, :TILE_ROWS, :] = jnp.zeros((TILE_ROWS, LANES), jnp.float32)
        out_ref[i, TILE_ROWS:, :] = jnp.full((8, LANES), -1.0, jnp.float32)
        return carry

    lax.fori_loop(0, peers * CAPD, clear, 0)

    def reset(i, carry):
        count_ref[i] = 0
        return carry

    lax.fori_loop(0, peers, reset, 0)

    def place(i, carry):
        entry = slots_ref[0, i]
        peer = entry // gshare
        rank = count_ref[peer]
        count_ref[peer] = rank + 1
        target = peer * CAPD + rank
        target_ref[i] = target
        out_ref[target, TILE_ROWS:, :] = jnp.full((8, LANES), (entry - peer * gshare).astype(jnp.float32))
        return carry

    lax.fori_loop(0, n_slots, place, 0)

    low_iota = lax.broadcasted_iota(jnp.int32, (LANES, LANES), 0).astype(jnp.float32).astype(jnp.bfloat16)
    high_iota = lax.broadcasted_iota(jnp.int32, (PIX_ROWS, LANES), 0).astype(jnp.float32).astype(jnp.bfloat16)
    one, zero = jnp.bfloat16(1.0), jnp.bfloat16(0.0)

    def strip(s, carry):
        lanes = pl.ds(pl.multiple_of(s * LANES, LANES), LANES)
        value = stream_ref[s]
        turn = angle_ref[0, :, lanes] * (1.0 / math.pi)
        turn = turn - jnp.round(turn)
        square = turn * turn
        parts = [value, value * horner(COS_FIT, square), value * turn * horner(SIN_FIT, square)]
        halves = [split_bf16(v) for v in parts]
        halves = [h[0] for h in halves] + [h[1] for h in halves]
        pix = pix_ref[0, :, lanes]
        high = (pix >> 7).astype(jnp.float32).astype(jnp.bfloat16)
        low = (pix & (LANES - 1)).astype(jnp.float32).astype(jnp.bfloat16)
        for d in range(dets):
            hit = high_iota == high[d : d + 1, :]
            rows = jnp.concatenate([jnp.where(hit, h[d : d + 1, :], zero) for h in halves], axis=0)
            spread = jnp.where(low_iota == low[d : d + 1, :], one, zero)
            both = lax.dot_general(rows, spread, (((1,), (1,)), ((), ())), preferred_element_type=jnp.float32)
            target = target_ref[tile_ref[0, d, s]]
            out_ref[target, :TILE_ROWS, :] += both[:TILE_ROWS] + both[TILE_ROWS:]
        return carry

    lax.fori_loop(0, strips, strip, 0)


def gather_kernel(n, n_tm, tiles_ref, home_ref, out_ref, got_ref, block_ref, homes_ref, owned_ref, det_sems, tm_sems):
    me, me_tm = lax.axis_index("det"), lax.axis_index("tm")
    gshare = home_ref.shape[1]
    barrier = pltpu.get_barrier_semaphore()
    for o in range(1, n):
        pl.semaphore_signal(barrier, inc=1, device_id={"det": lax.rem(me + o, n)}, device_id_type=pl.DeviceIdType.MESH)
    for o in range(1, n_tm):
        pl.semaphore_signal(barrier, inc=1, device_id={"tm": lax.rem(me_tm + o, n_tm)}, device_id_type=pl.DeviceIdType.MESH)
    pl.semaphore_wait(barrier, n + n_tm - 2)
    copies = []
    for o in range(1, n):
        peer = lax.rem(me + o, n)
        copy = remote(tiles_ref.at[pl.ds(peer * CAPD, CAPD)], got_ref.at[o], det_sems.at[0, o], det_sems.at[1, o],
                      {"det": peer})
        copy.start()
        copies.append(copy)
    got_ref[0] = tiles_ref[pl.ds(me * CAPD, CAPD)]
    for o in range(n):
        if o > 0:
            copies[o - 1].wait()
        for e in range(gshare):
            total = None if o == 0 else block_ref[e]
            for i in range(CAPD):
                label = got_ref[o, i, TILE_ROWS : TILE_ROWS + 1, :]
                term = jnp.where(label == float(e), got_ref[o, i, :TILE_ROWS, :], 0.0)
                total = term if total is None else total + term
            block_ref[e] = total
    codes = [jnp.full((1, LANES), home_ref[0, e], jnp.int32) for e in range(gshare)]
    owners = [code // OWN for code in codes]
    places = [code - owner * OWN for code, owner in zip(codes, owners)]
    ranks = []
    for e in range(gshare):
        rank = jnp.zeros((1, LANES), jnp.int32)
        for f in range(e):
            rank = rank + jnp.where(owners[f] == owners[e], 1, 0)
        ranks.append(rank)
    for peer in range(n_tm):
        for rank in range(CAPT):
            tile = jnp.zeros((TILE_ROWS, LANES), jnp.float32)
            label = jnp.full((1, LANES), -1, jnp.int32)
            for e in range(gshare):
                hit = jnp.where(owners[e] * CAPT + ranks[e] == peer * CAPT + rank, 1, 0)
                tile = jnp.where(hit == 1, block_ref[e], tile)
                label = jnp.where(hit == 1, places[e], label)
            homes_ref[peer * CAPT + rank, :TILE_ROWS, :] = tile
            homes_ref[peer * CAPT + rank, TILE_ROWS:, :] = jnp.broadcast_to(label.astype(jnp.float32), (8, LANES))
    copies = []
    for o in range(1, n_tm):
        peer = lax.rem(me_tm + o, n_tm)
        copy = remote(homes_ref.at[pl.ds(peer * CAPT, CAPT)], owned_ref.at[o], tm_sems.at[0, o], tm_sems.at[1, o],
                      {"tm": peer})
        copy.start()
        copies.append(copy)
    owned_ref[0] = homes_ref[pl.ds(me_tm * CAPT, CAPT)]
    for copy in copies:
        copy.wait()
    for t in range(OWN):
        for c in range(3):
            total = jnp.zeros((PIX_ROWS, LANES), jnp.float32)
            for o in range(n_tm):
                for i in range(CAPT):
                    label = owned_ref[o, i, TILE_ROWS : TILE_ROWS + 1, :]
                    part = owned_ref[o, i, c * PIX_ROWS : (c + 1) * PIX_ROWS, :]
                    total = total + jnp.where(label == float(t), part, 0.0)
            for h in range(PIX_ROWS):
                out_ref[t, c : c + 1, h * LANES : (h + 1) * LANES] = total[h : h + 1, :]


def per_device(timestream, polar_angle, pixel_index, strip_tile, time_const, knee_freq, noise_slope,
               white_weight, mode_mix, coupling, device_slots, slot_home):
    dets, total = timestream.shape[1:]
    scans = total // SAMPLES
    n_det, n_tm = lax.axis_size("det"), lax.axis_size("tm")
    matrices, rows = transform_tables()
    matrices, rows = jnp.asarray(matrices), jnp.asarray(rows)
    blocks = 2 * HALF
    share = blocks // n_det
    f32 = jnp.float32
    vmem = pl.BlockSpec(memory_space=pltpu.VMEM)
    smem = pl.BlockSpec(memory_space=pltpu.SMEM)
    stream = pl.pallas_call(
        functools.partial(clean_kernel, n_det),
        out_shape=jax.ShapeDtypeStruct((scans * OUTER, dets, LANES), f32),
        in_specs=[vmem] * 9,
        out_specs=vmem,
        scratch_shapes=[
            pltpu.VMEM((scans, blocks, dets, LANES), f32),
            pltpu.VMEM((scans, blocks, dets, LANES), f32),
            pltpu.VMEM((HALF + 1, dets, LANES), f32),
            pltpu.VMEM((HALF + 1, dets, LANES), f32),
            pltpu.VMEM((HALF * dets, 2 * LANES), f32),
            pltpu.VMEM((dets, LANES), f32),
            pltpu.VMEM((n_det, dets, LANES), f32),
            pltpu.VMEM((scans, n_det, share, dets, LANES), f32),
            pltpu.VMEM((scans, n_det, share, dets, LANES), f32),
            pltpu.SemaphoreType.DMA((2, n_det)),
            pltpu.SemaphoreType.DMA((2, scans, n_det)),
            pltpu.SemaphoreType.DMA((2, scans, n_det)),
        ],
        compiler_params=pltpu.CompilerParams(vmem_limit_bytes=VMEM_LIMIT, collective_id=1, has_side_effects=True),
        name="clean",
    )(timestream, time_const, knee_freq, noise_slope, white_weight, mode_mix, coupling, matrices, rows)
    tiles = pl.pallas_call(
        functools.partial(bin_kernel, slot_home.shape[1]),
        out_shape=jax.ShapeDtypeStruct((n_det * CAPD, SLOT_ROWS, LANES), f32),
        in_specs=[vmem] * 3 + [smem] * 2,
        out_specs=vmem,
        scratch_shapes=[pltpu.SMEM((device_slots.shape[1],), jnp.int32), pltpu.SMEM((n_det,), jnp.int32)],
        compiler_params=pltpu.CompilerParams(vmem_limit_bytes=VMEM_LIMIT),
        name="binning",
    )(stream, polar_angle, pixel_index, strip_tile, device_slots)
    return pl.pallas_call(
        functools.partial(gather_kernel, n_det, n_tm),
        out_shape=jax.ShapeDtypeStruct((OWN, 3, TILE_PIX), f32),
        in_specs=[vmem, smem],
        out_specs=vmem,
        scratch_shapes=[
            pltpu.VMEM((n_det, CAPD, SLOT_ROWS, LANES), f32),
            pltpu.VMEM((slot_home.shape[1], TILE_ROWS, LANES), f32),
            pltpu.VMEM((n_tm * CAPT, SLOT_ROWS, LANES), f32),
            pltpu.VMEM((n_tm, CAPT, SLOT_ROWS, LANES), f32),
            pltpu.SemaphoreType.DMA((2, n_det)),
            pltpu.SemaphoreType.DMA((2, n_tm)),
        ],
        compiler_params=pltpu.CompilerParams(vmem_limit_bytes=VMEM_LIMIT, collective_id=2, has_side_effects=True),
        name="gather",
    )(tiles, slot_home)


def solution(mesh):
    placed = (
        P("tm", "det", None),
        P("tm", "det", None),
        P("tm", "det", None),
        P("tm", "det", None),
        P("tm", "det"),
        P("tm", "det"),
        P("tm", "det"),
        P("tm", "det"),
        P("tm", "det", None),
        P(),
        P("tm", "det"),
        P("tm", "det"),
    )
    return jax.shard_map(
        per_device,
        mesh=mesh,
        in_specs=placed,
        out_specs=P(("tm", "det"), None, None),
        check_vma=False,
    )
```

```python
import functools
import math

import jax
import jax.numpy as jnp
import numpy as np
from jax import lax
from jax.experimental import pallas as pl
from jax.experimental.pallas import tpu as pltpu
from jax.sharding import PartitionSpec as P

SAMPLES = 4096
TILE_PIX = 2048
CAPD = 2
CAPT = 2
OWN = 8
LANES = 128
OUTER = SAMPLES // LANES
HALF = OUTER // 2
TILE_ROWS = 3 * TILE_PIX // LANES
PIX_ROWS = TILE_PIX // LANES
SLOT_ROWS = TILE_ROWS + 8

HIGHEST = lax.Precision.HIGHEST
VMEM_LIMIT = 56 * 1024 * 1024


def transform_tables():
    b = np.arange(LANES)[:, None]
    q = np.arange(LANES)[None, :]
    cos = np.cos(2 * np.pi * (b * q % LANES) / LANES)
    sin = np.sin(2 * np.pi * (b * q % LANES) / LANES)
    forward = np.block([[cos, -sin], [sin, cos]])
    backward = np.block([[cos, sin], [-sin, cos]]) / SAMPLES
    h = LANES // 2
    even_f = np.concatenate([cos[:, :h], -sin[:, :h]], axis=1)
    even_f[:, h] = cos[:, h]
    even_b = np.concatenate([2 * cos[:h], -2 * sin[:h]], axis=0)
    even_b[0] = 1.0
    even_b[h] = cos[h]
    odd_phase = 2 * np.pi * (b * (2 * np.arange(h)[None, :] + 1) % (2 * LANES)) / (2 * LANES)
    odd_f = np.concatenate([np.cos(odd_phase), -np.sin(odd_phase)], axis=1)
    odd_b = np.concatenate([2 * np.cos(odd_phase).T, -2 * np.sin(odd_phase).T], axis=0)
    zero = np.zeros((LANES, LANES))
    packed_f = np.block([[even_f, zero], [zero, odd_f]])
    packed_b = np.block([[even_b, zero], [zero, odd_b]]) / SAMPLES
    matrices = np.stack([packed_f, forward, packed_b, backward]).astype(np.float32)
    k1 = np.arange(HALF)[:, None]
    angle = 2 * np.pi * (k1 * q) / SAMPLES
    k = k1 + OUTER * q
    freq = (((k + SAMPLES // 2) % SAMPLES) - SAMPLES // 2) / SAMPLES
    lane = np.arange(LANES)
    low = lane % h
    even_k = OUTER * low
    even_k[h] = SAMPLES // 2
    odd_k = HALF + OUTER * low
    even_freq = (((even_k + SAMPLES // 2) % SAMPLES) - SAMPLES // 2) / SAMPLES
    odd_freq = (((odd_k + SAMPLES // 2) % SAMPLES) - SAMPLES // 2) / SAMPLES
    freq = np.concatenate([freq, odd_freq[None]], axis=0)
    freq[0] = even_freq
    with np.errstate(divide="ignore"):
        logs = np.where(freq == 0.0, -1e30, np.log2(np.abs(freq)))
    lag = 2 * np.pi * freq
    even_lag = np.where(lane < h, -lag[0], lag[0])
    even_lag[h] = 0.0
    even_lag[0] = 0.0
    odd_lag = np.where(lane < h, -lag[HALF], lag[HALF])
    lag[0] = even_lag
    lag[HALF] = odd_lag
    twist = np.stack([np.cos(angle), np.sin(angle)])
    rows = np.concatenate([twist[0], twist[1], logs, lag], axis=0)
    rows = np.concatenate([rows, np.zeros((-rows.shape[0] % 8, LANES))], axis=0)
    return matrices, rows.astype(np.float32)


ROW_COS, ROW_SIN, ROW_LOG, ROW_LAG = 0, HALF, 2 * HALF, 3 * HALF + 1


def add(x, y):
    return y if x is None else (x if y is None else x + y)


def sub(x, y):
    if y is None:
        return x
    return -y if x is None else x - y


def rotate(re, im, c, s):
    if abs(s) < 1e-12:
        return (re, im) if c > 0 else (-re, None if im is None else -im)
    if abs(c) < 1e-12:
        flip = None if im is None else (-im if s > 0 else im)
        return flip, (re if s > 0 else -re)
    if im is None:
        return re * c, re * s
    return re * c - im * s, im * c + re * s


def real_forward(xs):
    n = len(xs)
    if n == 1:
        return [xs[0]], [None]
    if n == 2:
        return [xs[0] + xs[1], xs[0] - xs[1]], [None, None]
    er, ei = real_forward(xs[0::2])
    odr, odi = real_forward(xs[1::2])
    re, im = [None] * (n // 2 + 1), [None] * (n // 2 + 1)
    for k in range(n // 4 + 1):
        angle = -2.0 * math.pi * k / n
        pr, pi_ = rotate(odr[k], odi[k], math.cos(angle), math.sin(angle))
        re[k], im[k] = add(er[k], pr), add(ei[k], pi_)
        if k < n // 4:
            re[n // 2 - k] = sub(er[k], pr)
            tail = sub(ei[k], pi_)
            im[n // 2 - k] = None if tail is None else -tail
    return re, im


def real_backward(re, im):
    n = 2 * (len(re) - 1)
    if n == 2:
        return [re[0] + re[1], re[0] - re[1]]
    er, ei, odr, odi = [], [], [], []
    for k in range(n // 4 + 1):
        m = n // 2 - k
        if k == 0:
            er.append(re[0] + re[m])
            ei.append(None)
            odr.append(re[0] - re[m])
            odi.append(None)
        elif k == m:
            er.append(2.0 * re[k])
            ei.append(None)
            odr.append(-2.0 * im[k])
            odi.append(None)
        else:
            er.append(re[k] + re[m])
            ei.append(im[k] - im[m])
            angle = 2.0 * math.pi * k / n
            pr, pi_ = rotate(re[k] - re[m], im[k] + im[m], math.cos(angle), math.sin(angle))
            odr.append(pr)
            odi.append(pi_)
    even, odd = real_backward(er, ei), real_backward(odr, odi)
    return [v for pair in zip(even, odd) for v in pair]


def split_bf16(x):
    high = x.astype(jnp.bfloat16)
    return high, (x - high.astype(jnp.float32)).astype(jnp.bfloat16)


def dot32(x, y):
    return jnp.dot(x, y, precision=HIGHEST, preferred_element_type=jnp.float32)


def column(row_ref, dets):
    wide = jnp.broadcast_to(row_ref[...], (dets, dets))
    own = lax.broadcasted_iota(jnp.int32, (dets, dets), 0) == lax.broadcasted_iota(jnp.int32, (dets, dets), 1)
    return jnp.sum(jnp.where(own, wide, 0.0), axis=1, keepdims=True)


def table_row(rows_ref, row, shape):
    return jnp.broadcast_to(rows_ref[row : row + 1, :], shape)


def noise_weights(tc_ref, knee_ref, slope_ref, white_ref, rows_ref, nw_ref, lag_ref):
    dets = tc_ref.shape[1]
    shape = (dets, LANES)
    slope, knee = column(slope_ref, dets), column(knee_ref, dets)
    knee_pow = jnp.broadcast_to(jnp.exp2(slope * jnp.log2(knee)), shape)
    slope = jnp.broadcast_to(slope, shape)
    tau, white = jnp.broadcast_to(column(tc_ref, dets), shape), jnp.broadcast_to(column(white_ref, dets), shape)
    for row in range(HALF + 1):
        power = jnp.exp2(slope * table_row(rows_ref, ROW_LOG + row, shape))
        nw_ref[row] = white * power / (power + knee_pow)
        lag_ref[row] = tau * table_row(rows_ref, ROW_LAG + row, shape)


def spectra(scan, ts_ref, mat_ref, rows_ref, nw_ref, lag_ref, work_ref, w_ref):
    dets = ts_ref.shape[1]
    for d0 in range(0, dets, 8):
        xs = [ts_ref[0, d0 : d0 + 8, (scan * OUTER + a) * LANES : (scan * OUTER + a + 1) * LANES] for a in range(OUTER)]
        re, im = real_forward(xs)
        for k1 in range(HALF):
            r = k1 * dets + d0
            if k1 == 0:
                out_re, out_im = re[0], re[HALF]
            else:
                c = table_row(rows_ref, ROW_COS + k1, (8, LANES))
                s = table_row(rows_ref, ROW_SIN + k1, (8, LANES))
                out_re, out_im = re[k1] * c + im[k1] * s, im[k1] * c - re[k1] * s
            work_ref[r : r + 8, :LANES] = out_re
            work_ref[r : r + 8, LANES:] = out_im
    work_ref[:dets, :] = dot32(work_ref[:dets, :], mat_ref[0])
    work_ref[dets:, :] = dot32(work_ref[dets:, :], mat_ref[1])
    for k1 in range(HALF):
        r = k1 * dets
        re, im = work_ref[r : r + dets, :LANES], work_ref[r : r + dets, LANES:]
        if k1 == 0:
            w_ref[scan, 0] = nw_ref[0] * (re + lag_ref[0] * pltpu.roll(re, LANES // 2, 1))
            w_ref[scan, HALF] = nw_ref[HALF] * (im + lag_ref[HALF] * pltpu.roll(im, LANES // 2, 1))
        else:
            w_ref[scan, k1] = nw_ref[k1] * (re - lag_ref[k1] * im)
            w_ref[scan, HALF + k1] = nw_ref[k1] * (im + lag_ref[k1] * re)


def streams(scan, w_ref, p_ref, nw_ref, mat_ref, rows_ref, work_ref, turns_ref, out_ref):
    dets = w_ref.shape[2]
    for part in range(2):
        for k1 in range(HALF):
            row = HALF if (part == 1 and k1 == 0) else k1
            i = part * HALF + k1
            r = k1 * dets
            work_ref[r : r + dets, part * LANES : (part + 1) * LANES] = w_ref[scan, i] - nw_ref[row] * p_ref[scan, i]
    work_ref[:dets, :] = dot32(work_ref[:dets, :], mat_ref[2])
    work_ref[dets:, :] = dot32(work_ref[dets:, :], mat_ref[3])
    for d0 in range(0, dets, 8):
        re, im = [], []
        for k1 in range(HALF):
            r = k1 * dets + d0
            zr, zi = work_ref[r : r + 8, :LANES], work_ref[r : r + 8, LANES:]
            if k1 == 0:
                re.append(zr)
                im.append(None)
                last = zi
            else:
                c = table_row(rows_ref, ROW_COS + k1, (8, LANES))
                s = table_row(rows_ref, ROW_SIN + k1, (8, LANES))
                re.append(zr * c - zi * s)
                im.append(zi * c + zr * s)
        re.append(last)
        im.append(None)
        for a, value in enumerate(real_backward(re, im)):
            s = scan * OUTER + a
            out_ref[s, 0, d0 : d0 + 8, :] = value
            out_ref[s, 1, d0 : d0 + 8, :] = value * turns_ref[s, 0, d0 : d0 + 8, :]
            out_ref[s, 2, d0 : d0 + 8, :] = value * turns_ref[s, 1, d0 : d0 + 8, :]


def turn_polynomials():
    x = (np.cos(np.pi * (np.arange(400) + 0.5) / 400) + 1) / 8
    t = np.sqrt(x)
    cheb = np.polynomial.Polynomial
    cos_fit = cheb.fit(x, np.cos(2 * np.pi * t), 7).convert().coef
    sin_fit = cheb.fit(x, np.sin(2 * np.pi * t) / t, 7).convert().coef
    return [float(np.float32(c)) for c in cos_fit], [float(np.float32(c)) for c in sin_fit]


COS_FIT, SIN_FIT = turn_polynomials()


def horner(coefficients, x):
    total = jnp.full_like(x, coefficients[-1])
    for c in coefficients[-2::-1]:
        total = total * x + c
    return total


def turn_angles(scan, angle_ref, turns_ref):
    for a in range(scan * OUTER, (scan + 1) * OUTER):
        turn = angle_ref[0, :, a * LANES : (a + 1) * LANES] * (1.0 / math.pi)
        turn = turn - jnp.round(turn)
        square = turn * turn
        turns_ref[a, 0] = horner(COS_FIT, square)
        turns_ref[a, 1] = turn * horner(SIN_FIT, square)


def remote(src, dst, send_sem, recv_sem, device):
    return pltpu.make_async_remote_copy(
        src_ref=src, dst_ref=dst, send_sem=send_sem, recv_sem=recv_sem, device_id=device,
        device_id_type=pl.DeviceIdType.MESH,
    )


def clean_kernel(n, ts_ref, angle_ref, tc_ref, knee_ref, slope_ref, white_ref, mix_ref, cpl_ref, mat_ref, rows_ref, out_ref,
                 w_ref, p_ref, nw_ref, lag_ref, work_ref, turns_ref, mine_ref, mix_all_ref, got_ref, back_ref,
                 mix_sems, out_sems, back_sems):
    me = lax.axis_index("det")
    scans, rows_all, dets, _ = w_ref.shape
    share = rows_all // n
    modes = mix_ref.shape[2]
    offsets = range(1, n)
    ahead = [lax.rem(me + o, n) for o in range(n)]
    behind = [lax.rem(me + n - o, n) for o in range(n)]
    barrier = pltpu.get_barrier_semaphore()
    for o in offsets:
        pl.semaphore_signal(barrier, inc=1, device_id={"det": ahead[o]}, device_id_type=pl.DeviceIdType.MESH)
    pl.semaphore_wait(barrier, n - 1)
    mine = jnp.concatenate([mix_ref[0], jnp.zeros((dets, LANES - modes), jnp.float32)], axis=1)
    mine_ref[...] = mine
    mix_all_ref[0] = mine
    copies = []
    for o in offsets:
        copy = remote(mine_ref, mix_all_ref.at[o], mix_sems.at[0, o], mix_sems.at[1, o], {"det": ahead[o]})
        copy.start()
        copies.append(copy)
    noise_weights(tc_ref, knee_ref, slope_ref, white_ref, rows_ref, nw_ref, lag_ref)
    outgoing = []
    for scan in range(scans):
        spectra(scan, ts_ref, mat_ref, rows_ref, nw_ref, lag_ref, work_ref, w_ref)
        sent = []
        for o in offsets:
            copy = remote(w_ref.at[scan, pl.ds(ahead[o] * share, share)], got_ref.at[scan, o],
                          out_sems.at[0, scan, o], out_sems.at[1, scan, o], {"det": ahead[o]})
            copy.start()
            sent.append(copy)
        outgoing.append(sent)
        got_ref[scan, 0] = w_ref[scan, pl.ds(me * share, share)]
    for copy in copies:
        copy.wait()
    mix = jnp.concatenate([mix_all_ref[o] for o in range(n)], axis=0)[:, :modes]
    gram = lax.dot_general(dot32(mix, cpl_ref[...]), mix, (((1,), (1,)), ((), ())), precision=HIGHEST,
                           preferred_element_type=jnp.float32)
    returning = []
    for scan in range(scans):
        turn_angles(scan, angle_ref, turns_ref)
        for copy in outgoing[scan]:
            copy.wait()
        for r in range(share):
            block = jnp.concatenate([got_ref[scan, o, r] for o in range(n)], axis=0)
            back = dot32(gram, block)
            for o in range(n):
                back_ref[scan, o, r] = back[o * dets : (o + 1) * dets]
        sent = []
        for o in offsets:
            copy = remote(back_ref.at[scan, o], p_ref.at[scan, pl.ds(me * share, share)],
                          back_sems.at[0, scan, o], back_sems.at[1, scan, o], {"det": behind[o]})
            copy.start()
            sent.append(copy)
        returning.append(sent)
        p_ref[scan, pl.ds(me * share, share)] = back_ref[scan, 0]
    for scan in range(scans):
        for copy in returning[scan]:
            copy.wait()
        streams(scan, w_ref, p_ref, nw_ref, mat_ref, rows_ref, work_ref, turns_ref, out_ref)


def bin_kernel(gshare, stream_ref, pix_ref, tile_ref, slots_ref, out_ref, rows_ref, target_ref, count_ref):
    strips, _, dets, _ = stream_ref.shape
    n_slots = slots_ref.shape[1]
    peers = out_ref.shape[0] // CAPD

    def clear(i, carry):
        out_ref[i, :TILE_ROWS, :] = jnp.zeros((TILE_ROWS, LANES), jnp.float32)
        out_ref[i, TILE_ROWS:, :] = jnp.full((8, LANES), -1.0, jnp.float32)
        return carry

    lax.fori_loop(0, peers * CAPD, clear, 0)

    def reset(i, carry):
        count_ref[i] = 0
        return carry

    lax.fori_loop(0, peers, reset, 0)

    def place(i, carry):
        entry = slots_ref[0, i]
        peer = entry // gshare
        rank = count_ref[peer]
        count_ref[peer] = rank + 1
        target = peer * CAPD + rank
        target_ref[i] = target
        out_ref[target, TILE_ROWS:, :] = jnp.full((8, LANES), (entry - peer * gshare).astype(jnp.float32))
        return carry

    lax.fori_loop(0, n_slots, place, 0)

    low_iota = lax.broadcasted_iota(jnp.int32, (LANES, LANES), 0).astype(jnp.float32).astype(jnp.bfloat16)
    high_iota = lax.broadcasted_iota(jnp.int32, (PIX_ROWS, LANES), 0).astype(jnp.float32).astype(jnp.bfloat16)
    one, zero = jnp.bfloat16(1.0), jnp.bfloat16(0.0)
    blank = jnp.zeros((LANES, LANES), jnp.bfloat16)

    def prepare(s, carry):
        lanes = pl.ds(pl.multiple_of(s * LANES, LANES), LANES)
        for c in range(3):
            value = stream_ref[s, c]
            high = value.astype(jnp.bfloat16).astype(jnp.float32)
            rows_ref[s, c] = high
            rows_ref[s, 3 + c] = value - high
        pix = pix_ref[0, :, lanes]
        rows_ref[s, 6] = (pix >> 7).astype(jnp.float32)
        rows_ref[s, 7] = (pix & (LANES - 1)).astype(jnp.float32)
        return carry

    lax.fori_loop(0, strips, prepare, 0, unroll=4)

    def wide(s, i, d):
        return jnp.broadcast_to(rows_ref[s, i, d : d + 1, :], (16, LANES)).astype(jnp.bfloat16)

    def strip(s, carry):
        for d0 in range(0, dets, 2):
            rows, spreads = [], []
            for d in (d0, d0 + 1):
                hit = high_iota == wide(s, 6, d)
                rows.append(jnp.concatenate([jnp.where(hit, wide(s, i, d), zero) for i in range(6)], axis=0))
                low = wide(s, 7, d)
                spreads.append(jnp.concatenate(
                    [jnp.where(low_iota[r : r + 16] == low, one, zero) for r in range(0, LANES, 16)], axis=0))
            spread = jnp.concatenate([
                jnp.concatenate([spreads[0], blank], axis=1), jnp.concatenate([blank, spreads[1]], axis=1)], axis=0)
            both = lax.dot_general(jnp.concatenate(rows, axis=1), spread, (((1,), (1,)), ((), ())),
                                   preferred_element_type=jnp.float32)
            both = both[:TILE_ROWS] + both[TILE_ROWS:]
            for d in (d0, d0 + 1):
                target = target_ref[tile_ref[0, d, s]]
                out_ref[target, :TILE_ROWS, :] += both[:, (d - d0) * LANES : (d - d0 + 1) * LANES]
        return carry

    lax.fori_loop(0, strips, strip, 0)


def gather_kernel(n, n_tm, tiles_ref, home_ref, owned_ref, got_ref, block_ref, homes_ref, det_sems, tm_sems):
    me, me_tm = lax.axis_index("det"), lax.axis_index("tm")
    gshare = home_ref.shape[1]
    barrier = pltpu.get_barrier_semaphore()
    for o in range(1, n):
        pl.semaphore_signal(barrier, inc=1, device_id={"det": lax.rem(me + o, n)}, device_id_type=pl.DeviceIdType.MESH)
    for o in range(1, n_tm):
        pl.semaphore_signal(barrier, inc=1, device_id={"tm": lax.rem(me_tm + o, n_tm)}, device_id_type=pl.DeviceIdType.MESH)
    pl.semaphore_wait(barrier, n + n_tm - 2)
    copies = []
    for o in range(1, n):
        peer = lax.rem(me + o, n)
        copy = remote(tiles_ref.at[pl.ds(peer * CAPD, CAPD)], got_ref.at[o], det_sems.at[0, o], det_sems.at[1, o],
                      {"det": peer})
        copy.start()
        copies.append(copy)
    got_ref[0] = tiles_ref[pl.ds(me * CAPD, CAPD)]
    for o in range(n):
        if o > 0:
            copies[o - 1].wait()
        for e in range(gshare):
            total = None if o == 0 else block_ref[e]
            for i in range(CAPD):
                label = got_ref[o, i, TILE_ROWS : TILE_ROWS + 1, :]
                term = jnp.where(label == float(e), got_ref[o, i, :TILE_ROWS, :], 0.0)
                total = term if total is None else total + term
            block_ref[e] = total
    codes = [jnp.full((1, LANES), home_ref[0, e], jnp.int32) for e in range(gshare)]
    owners = [code // OWN for code in codes]
    places = [code - owner * OWN for code, owner in zip(codes, owners)]
    ranks = []
    for e in range(gshare):
        rank = jnp.zeros((1, LANES), jnp.int32)
        for f in range(e):
            rank = rank + jnp.where(owners[f] == owners[e], 1, 0)
        ranks.append(rank)
    for peer in range(n_tm):
        for rank in range(CAPT):
            tile = jnp.zeros((TILE_ROWS, LANES), jnp.float32)
            label = jnp.full((1, LANES), -1, jnp.int32)
            for e in range(gshare):
                hit = jnp.where(owners[e] * CAPT + ranks[e] == peer * CAPT + rank, 1, 0)
                tile = jnp.where(hit == 1, block_ref[e], tile)
                label = jnp.where(hit == 1, places[e], label)
            homes_ref[peer * CAPT + rank, :TILE_ROWS, :] = tile
            homes_ref[peer * CAPT + rank, TILE_ROWS:, :] = jnp.broadcast_to(label.astype(jnp.float32), (8, LANES))
    copies = []
    for o in range(1, n_tm):
        peer = lax.rem(me_tm + o, n_tm)
        copy = remote(homes_ref.at[pl.ds(peer * CAPT, CAPT)], owned_ref.at[o], tm_sems.at[0, o], tm_sems.at[1, o],
                      {"tm": peer})
        copy.start()
        copies.append(copy)
    owned_ref[0] = homes_ref[pl.ds(me_tm * CAPT, CAPT)]
    for copy in copies:
        copy.wait()


def place_kernel(owned_ref, out_ref):
    n_tm = owned_ref.shape[0]
    for t in range(OWN):
        for c in range(3):
            total = jnp.zeros((PIX_ROWS, LANES), jnp.float32)
            for o in range(n_tm):
                for i in range(CAPT):
                    label = owned_ref[o, i, TILE_ROWS : TILE_ROWS + 1, :]
                    part = owned_ref[o, i, c * PIX_ROWS : (c + 1) * PIX_ROWS, :]
                    total = total + jnp.where(label == float(t), part, 0.0)
            for h in range(PIX_ROWS):
                out_ref[c, t : t + 1, h * LANES : (h + 1) * LANES] = total[h : h + 1, :]


def per_device(timestream, polar_angle, pixel_index, strip_tile, time_const, knee_freq, noise_slope,
               white_weight, mode_mix, coupling, device_slots, slot_home):
    dets, total = timestream.shape[1:]
    scans = total // SAMPLES
    n_det, n_tm = lax.axis_size("det"), lax.axis_size("tm")
    matrices, rows = transform_tables()
    matrices, rows = jnp.asarray(matrices), jnp.asarray(rows)
    blocks = 2 * HALF
    share = blocks // n_det
    f32 = jnp.float32
    vmem = pl.BlockSpec(memory_space=pltpu.VMEM)
    smem = pl.BlockSpec(memory_space=pltpu.SMEM)
    stream = pl.pallas_call(
        functools.partial(clean_kernel, n_det),
        out_shape=jax.ShapeDtypeStruct((scans * OUTER, 3, dets, LANES), f32),
        in_specs=[vmem] * 10,
        out_specs=vmem,
        scratch_shapes=[
            pltpu.VMEM((scans, blocks, dets, LANES), f32),
            pltpu.VMEM((scans, blocks, dets, LANES), f32),
            pltpu.VMEM((HALF + 1, dets, LANES), f32),
            pltpu.VMEM((HALF + 1, dets, LANES), f32),
            pltpu.VMEM((HALF * dets, 2 * LANES), f32),
            pltpu.VMEM((scans * OUTER, 2, dets, LANES), f32),
            pltpu.VMEM((dets, LANES), f32),
            pltpu.VMEM((n_det, dets, LANES), f32),
            pltpu.VMEM((scans, n_det, share, dets, LANES), f32),
            pltpu.VMEM((scans, n_det, share, dets, LANES), f32),
            pltpu.SemaphoreType.DMA((2, n_det)),
            pltpu.SemaphoreType.DMA((2, scans, n_det)),
            pltpu.SemaphoreType.DMA((2, scans, n_det)),
        ],
        compiler_params=pltpu.CompilerParams(vmem_limit_bytes=VMEM_LIMIT, collective_id=1, has_side_effects=True),
        name="clean",
    )(timestream, polar_angle, time_const, knee_freq, noise_slope, white_weight, mode_mix, coupling, matrices, rows)
    tiles = pl.pallas_call(
        functools.partial(bin_kernel, slot_home.shape[1]),
        out_shape=jax.ShapeDtypeStruct((n_det * CAPD, SLOT_ROWS, LANES), f32),
        in_specs=[vmem] * 2 + [smem] * 2,
        out_specs=vmem,
        scratch_shapes=[pltpu.VMEM((scans * OUTER, 8, dets, LANES), f32), pltpu.SMEM((device_slots.shape[1],), jnp.int32), pltpu.SMEM((n_det,), jnp.int32)],
        compiler_params=pltpu.CompilerParams(vmem_limit_bytes=VMEM_LIMIT),
        name="binning",
    )(stream, pixel_index, strip_tile, device_slots)
    owned = pl.pallas_call(
        functools.partial(gather_kernel, n_det, n_tm),
        out_shape=jax.ShapeDtypeStruct((n_tm, CAPT, SLOT_ROWS, LANES), f32),
        in_specs=[vmem, smem],
        out_specs=vmem,
        scratch_shapes=[
            pltpu.VMEM((n_det, CAPD, SLOT_ROWS, LANES), f32),
            pltpu.VMEM((slot_home.shape[1], TILE_ROWS, LANES), f32),
            pltpu.VMEM((n_tm * CAPT, SLOT_ROWS, LANES), f32),
            pltpu.SemaphoreType.DMA((2, n_det)),
            pltpu.SemaphoreType.DMA((2, n_tm)),
        ],
        compiler_params=pltpu.CompilerParams(vmem_limit_bytes=VMEM_LIMIT, collective_id=2, has_side_effects=True),
        name="gather",
    )(tiles, slot_home)
    out = pl.pallas_call(
        place_kernel,
        out_shape=jax.ShapeDtypeStruct((3, OWN, TILE_PIX), f32),
        in_specs=[vmem],
        out_specs=vmem,
        compiler_params=pltpu.CompilerParams(vmem_limit_bytes=VMEM_LIMIT),
        name="place",
    )(owned)
    return jnp.transpose(out, (1, 0, 2))


def solution(mesh):
    placed = (
        P("tm", "det", None),
        P("tm", "det", None),
        P("tm", "det", None),
        P("tm", "det", None),
        P("tm", "det"),
        P("tm", "det"),
        P("tm", "det"),
        P("tm", "det"),
        P("tm", "det", None),
        P(),
        P("tm", "det"),
        P("tm", "det"),
    )
    return jax.shard_map(
        per_device,
        mesh=mesh,
        in_specs=placed,
        out_specs=P(("tm", "det"), None, None),
        check_vma=False,
    )
```

```python
import functools
import math

import jax
import jax.numpy as jnp
import numpy as np
from jax import lax
from jax.experimental import pallas as pl
from jax.experimental.pallas import tpu as pltpu
from jax.sharding import PartitionSpec as P

SAMPLES = 4096
TILE_PIX = 2048
CAPD = 2
CAPT = 2
OWN = 8
LANES = 128
OUTER = SAMPLES // LANES
HALF = OUTER // 2
TILE_ROWS = 3 * TILE_PIX // LANES
PIX_ROWS = TILE_PIX // LANES
SLOT_ROWS = TILE_ROWS + 8

HIGHEST = lax.Precision.HIGHEST
VMEM_LIMIT = 56 * 1024 * 1024


def transform_tables():
    b = np.arange(LANES)[:, None]
    q = np.arange(LANES)[None, :]
    cos = np.cos(2 * np.pi * (b * q % LANES) / LANES)
    sin = np.sin(2 * np.pi * (b * q % LANES) / LANES)
    forward = np.block([[cos, -sin], [sin, cos]])
    backward = np.block([[cos, sin], [-sin, cos]]) / SAMPLES
    h = LANES // 2
    even_f = np.concatenate([cos[:, :h], -sin[:, :h]], axis=1)
    even_f[:, h] = cos[:, h]
    even_b = np.concatenate([2 * cos[:h], -2 * sin[:h]], axis=0)
    even_b[0] = 1.0
    even_b[h] = cos[h]
    odd_phase = 2 * np.pi * (b * (2 * np.arange(h)[None, :] + 1) % (2 * LANES)) / (2 * LANES)
    odd_f = np.concatenate([np.cos(odd_phase), -np.sin(odd_phase)], axis=1)
    odd_b = np.concatenate([2 * np.cos(odd_phase).T, -2 * np.sin(odd_phase).T], axis=0)
    zero = np.zeros((LANES, LANES))
    packed_f = np.block([[even_f, zero], [zero, odd_f]])
    packed_b = np.block([[even_b, zero], [zero, odd_b]]) / SAMPLES
    matrices = np.stack([packed_f, forward, packed_b, backward]).astype(np.float32)
    k1 = np.arange(HALF)[:, None]
    angle = 2 * np.pi * (k1 * q) / SAMPLES
    k = k1 + OUTER * q
    freq = (((k + SAMPLES // 2) % SAMPLES) - SAMPLES // 2) / SAMPLES
    lane = np.arange(LANES)
    low = lane % h
    even_k = OUTER * low
    even_k[h] = SAMPLES // 2
    odd_k = HALF + OUTER * low
    even_freq = (((even_k + SAMPLES // 2) % SAMPLES) - SAMPLES // 2) / SAMPLES
    odd_freq = (((odd_k + SAMPLES // 2) % SAMPLES) - SAMPLES // 2) / SAMPLES
    freq = np.concatenate([freq, odd_freq[None]], axis=0)
    freq[0] = even_freq
    with np.errstate(divide="ignore"):
        logs = np.where(freq == 0.0, -1e30, np.log2(np.abs(freq)))
    lag = 2 * np.pi * freq
    even_lag = np.where(lane < h, -lag[0], lag[0])
    even_lag[h] = 0.0
    even_lag[0] = 0.0
    odd_lag = np.where(lane < h, -lag[HALF], lag[HALF])
    lag[0] = even_lag
    lag[HALF] = odd_lag
    twist = np.stack([np.cos(angle), np.sin(angle)])
    rows = np.concatenate([twist[0], twist[1], logs, lag], axis=0)
    rows = np.concatenate([rows, np.zeros((-rows.shape[0] % 8, LANES))], axis=0)
    return matrices, rows.astype(np.float32)


ROW_COS, ROW_SIN, ROW_LOG, ROW_LAG = 0, HALF, 2 * HALF, 3 * HALF + 1


def add(x, y):
    return y if x is None else (x if y is None else x + y)


def sub(x, y):
    if y is None:
        return x
    return -y if x is None else x - y


def rotate(re, im, c, s):
    if abs(s) < 1e-12:
        return (re, im) if c > 0 else (-re, None if im is None else -im)
    if abs(c) < 1e-12:
        flip = None if im is None else (-im if s > 0 else im)
        return flip, (re if s > 0 else -re)
    if im is None:
        return re * c, re * s
    return re * c - im * s, im * c + re * s


def real_forward(xs):
    n = len(xs)
    if n == 1:
        return [xs[0]], [None]
    if n == 2:
        return [xs[0] + xs[1], xs[0] - xs[1]], [None, None]
    er, ei = real_forward(xs[0::2])
    odr, odi = real_forward(xs[1::2])
    re, im = [None] * (n // 2 + 1), [None] * (n // 2 + 1)
    for k in range(n // 4 + 1):
        angle = -2.0 * math.pi * k / n
        pr, pi_ = rotate(odr[k], odi[k], math.cos(angle), math.sin(angle))
        re[k], im[k] = add(er[k], pr), add(ei[k], pi_)
        if k < n // 4:
            re[n // 2 - k] = sub(er[k], pr)
            tail = sub(ei[k], pi_)
            im[n // 2 - k] = None if tail is None else -tail
    return re, im


def real_backward(re, im):
    n = 2 * (len(re) - 1)
    if n == 2:
        return [re[0] + re[1], re[0] - re[1]]
    er, ei, odr, odi = [], [], [], []
    for k in range(n // 4 + 1):
        m = n // 2 - k
        if k == 0:
            er.append(re[0] + re[m])
            ei.append(None)
            odr.append(re[0] - re[m])
            odi.append(None)
        elif k == m:
            er.append(2.0 * re[k])
            ei.append(None)
            odr.append(-2.0 * im[k])
            odi.append(None)
        else:
            er.append(re[k] + re[m])
            ei.append(im[k] - im[m])
            angle = 2.0 * math.pi * k / n
            pr, pi_ = rotate(re[k] - re[m], im[k] + im[m], math.cos(angle), math.sin(angle))
            odr.append(pr)
            odi.append(pi_)
    even, odd = real_backward(er, ei), real_backward(odr, odi)
    return [v for pair in zip(even, odd) for v in pair]


def split_bf16(x):
    high = x.astype(jnp.bfloat16)
    return high, (x - high.astype(jnp.float32)).astype(jnp.bfloat16)


def dot32(x, y):
    return jnp.dot(x, y, precision=HIGHEST, preferred_element_type=jnp.float32)


def column(row_ref, dets):
    wide = jnp.broadcast_to(row_ref[...], (dets, dets))
    own = lax.broadcasted_iota(jnp.int32, (dets, dets), 0) == lax.broadcasted_iota(jnp.int32, (dets, dets), 1)
    return jnp.sum(jnp.where(own, wide, 0.0), axis=1, keepdims=True)


def table_row(rows_ref, row, shape):
    return jnp.broadcast_to(rows_ref[row : row + 1, :], shape)


def noise_weights(tc_ref, knee_ref, slope_ref, white_ref, rows_ref, nw_ref, lag_ref):
    dets = tc_ref.shape[1]
    shape = (dets, LANES)
    slope, knee = column(slope_ref, dets), column(knee_ref, dets)
    knee_pow = jnp.broadcast_to(jnp.exp2(slope * jnp.log2(knee)), shape)
    slope = jnp.broadcast_to(slope, shape)
    tau, white = jnp.broadcast_to(column(tc_ref, dets), shape), jnp.broadcast_to(column(white_ref, dets), shape)
    for row in range(HALF + 1):
        power = jnp.exp2(slope * table_row(rows_ref, ROW_LOG + row, shape))
        nw_ref[row] = white * power / (power + knee_pow)
        lag_ref[row] = tau * table_row(rows_ref, ROW_LAG + row, shape)


def spectra(scan, ts_ref, mat_ref, rows_ref, nw_ref, lag_ref, work_ref, w_ref):
    dets = ts_ref.shape[1]
    for d0 in range(0, dets, 8):
        xs = [ts_ref[0, d0 : d0 + 8, (scan * OUTER + a) * LANES : (scan * OUTER + a + 1) * LANES] for a in range(OUTER)]
        re, im = real_forward(xs)
        for k1 in range(HALF):
            r = k1 * dets + d0
            if k1 == 0:
                out_re, out_im = re[0], re[HALF]
            else:
                c = table_row(rows_ref, ROW_COS + k1, (8, LANES))
                s = table_row(rows_ref, ROW_SIN + k1, (8, LANES))
                out_re, out_im = re[k1] * c + im[k1] * s, im[k1] * c - re[k1] * s
            work_ref[r : r + 8, :LANES] = out_re
            work_ref[r : r + 8, LANES:] = out_im
    work_ref[:dets, :] = dot32(work_ref[:dets, :], mat_ref[0])
    work_ref[dets:, :] = dot32(work_ref[dets:, :], mat_ref[1])
    for k1 in range(HALF):
        r = k1 * dets
        re, im = work_ref[r : r + dets, :LANES], work_ref[r : r + dets, LANES:]
        if k1 == 0:
            w_ref[scan, 0] = nw_ref[0] * (re + lag_ref[0] * pltpu.roll(re, LANES // 2, 1))
            w_ref[scan, HALF] = nw_ref[HALF] * (im + lag_ref[HALF] * pltpu.roll(im, LANES // 2, 1))
        else:
            w_ref[scan, k1] = nw_ref[k1] * (re - lag_ref[k1] * im)
            w_ref[scan, HALF + k1] = nw_ref[k1] * (im + lag_ref[k1] * re)


def streams(scan, w_ref, p_ref, nw_ref, mat_ref, rows_ref, work_ref, turns_ref, out_ref):
    dets = w_ref.shape[2]
    for part in range(2):
        for k1 in range(HALF):
            row = HALF if (part == 1 and k1 == 0) else k1
            i = part * HALF + k1
            r = k1 * dets
            work_ref[r : r + dets, part * LANES : (part + 1) * LANES] = w_ref[scan, i] - nw_ref[row] * p_ref[scan, i]
    work_ref[:dets, :] = dot32(work_ref[:dets, :], mat_ref[2])
    work_ref[dets:, :] = dot32(work_ref[dets:, :], mat_ref[3])
    for d0 in range(0, dets, 8):
        re, im = [], []
        for k1 in range(HALF):
            r = k1 * dets + d0
            zr, zi = work_ref[r : r + 8, :LANES], work_ref[r : r + 8, LANES:]
            if k1 == 0:
                re.append(zr)
                im.append(None)
                last = zi
            else:
                c = table_row(rows_ref, ROW_COS + k1, (8, LANES))
                s = table_row(rows_ref, ROW_SIN + k1, (8, LANES))
                re.append(zr * c - zi * s)
                im.append(zi * c + zr * s)
        re.append(last)
        im.append(None)
        for a, value in enumerate(real_backward(re, im)):
            s = scan * OUTER + a
            out_ref[s, 0, d0 : d0 + 8, :] = value
            out_ref[s, 1, d0 : d0 + 8, :] = value * turns_ref[s, 0, d0 : d0 + 8, :]
            out_ref[s, 2, d0 : d0 + 8, :] = value * turns_ref[s, 1, d0 : d0 + 8, :]


def turn_polynomials():
    x = (np.cos(np.pi * (np.arange(400) + 0.5) / 400) + 1) / 8
    t = np.sqrt(x)
    cheb = np.polynomial.Polynomial
    cos_fit = cheb.fit(x, np.cos(2 * np.pi * t), 7).convert().coef
    sin_fit = cheb.fit(x, np.sin(2 * np.pi * t) / t, 7).convert().coef
    return [float(np.float32(c)) for c in cos_fit], [float(np.float32(c)) for c in sin_fit]


COS_FIT, SIN_FIT = turn_polynomials()


def horner(coefficients, x):
    total = jnp.full_like(x, coefficients[-1])
    for c in coefficients[-2::-1]:
        total = total * x + c
    return total


def turn_angles(scan, angle_ref, turns_ref):
    for a in range(scan * OUTER, (scan + 1) * OUTER):
        turn = angle_ref[0, :, a * LANES : (a + 1) * LANES] * (1.0 / math.pi)
        turn = turn - jnp.round(turn)
        square = turn * turn
        turns_ref[a, 0] = horner(COS_FIT, square)
        turns_ref[a, 1] = turn * horner(SIN_FIT, square)


def remote(src, dst, send_sem, recv_sem, device):
    return pltpu.make_async_remote_copy(
        src_ref=src, dst_ref=dst, send_sem=send_sem, recv_sem=recv_sem, device_id=device,
        device_id_type=pl.DeviceIdType.MESH,
    )


def clean_kernel(n, ts_ref, angle_ref, tc_ref, knee_ref, slope_ref, white_ref, mix_ref, cpl_ref, mat_ref, rows_ref, out_ref,
                 w_ref, p_ref, nw_ref, lag_ref, work_ref, turns_ref, mine_ref, mix_all_ref, got_ref, back_ref,
                 mix_sems, out_sems, back_sems):
    me = lax.axis_index("det")
    scans, rows_all, dets, _ = w_ref.shape
    share = rows_all // n
    modes = mix_ref.shape[2]
    offsets = range(1, n)
    ahead = [lax.rem(me + o, n) for o in range(n)]
    behind = [lax.rem(me + n - o, n) for o in range(n)]
    barrier = pltpu.get_barrier_semaphore()
    for o in offsets:
        pl.semaphore_signal(barrier, inc=1, device_id={"det": ahead[o]}, device_id_type=pl.DeviceIdType.MESH)
    pl.semaphore_wait(barrier, n - 1)
    mine = jnp.concatenate([mix_ref[0], jnp.zeros((dets, LANES - modes), jnp.float32)], axis=1)
    mine_ref[...] = mine
    mix_all_ref[0] = mine
    copies = []
    for o in offsets:
        copy = remote(mine_ref, mix_all_ref.at[o], mix_sems.at[0, o], mix_sems.at[1, o], {"det": ahead[o]})
        copy.start()
        copies.append(copy)
    noise_weights(tc_ref, knee_ref, slope_ref, white_ref, rows_ref, nw_ref, lag_ref)
    outgoing = []
    for scan in range(scans):
        spectra(scan, ts_ref, mat_ref, rows_ref, nw_ref, lag_ref, work_ref, w_ref)
        sent = []
        for o in offsets:
            copy = remote(w_ref.at[scan, pl.ds(ahead[o] * share, share)], got_ref.at[scan, o],
                          out_sems.at[0, scan, o], out_sems.at[1, scan, o], {"det": ahead[o]})
            copy.start()
            sent.append(copy)
        outgoing.append(sent)
        got_ref[scan, 0] = w_ref[scan, pl.ds(me * share, share)]
    for copy in copies:
        copy.wait()
    mix = jnp.concatenate([mix_all_ref[o] for o in range(n)], axis=0)[:, :modes]
    gram = lax.dot_general(dot32(mix, cpl_ref[...]), mix, (((1,), (1,)), ((), ())), precision=HIGHEST,
                           preferred_element_type=jnp.float32)
    returning = []
    for scan in range(scans):
        turn_angles(scan, angle_ref, turns_ref)
        for copy in outgoing[scan]:
            copy.wait()
        for r in range(share):
            block = jnp.concatenate([got_ref[scan, o, r] for o in range(n)], axis=0)
            back = dot32(gram, block)
            for o in range(n):
                back_ref[scan, o, r] = back[o * dets : (o + 1) * dets]
        sent = []
        for o in offsets:
            copy = remote(back_ref.at[scan, o], p_ref.at[scan, pl.ds(me * share, share)],
                          back_sems.at[0, scan, o], back_sems.at[1, scan, o], {"det": behind[o]})
            copy.start()
            sent.append(copy)
        returning.append(sent)
        p_ref[scan, pl.ds(me * share, share)] = back_ref[scan, 0]
    for scan in range(scans):
        for copy in returning[scan]:
            copy.wait()
        streams(scan, w_ref, p_ref, nw_ref, mat_ref, rows_ref, work_ref, turns_ref, out_ref)


def bin_kernel(gshare, stream_ref, pix_ref, tile_ref, slots_ref, out_ref, rows_ref, target_ref, count_ref):
    strips, _, dets, _ = stream_ref.shape
    n_slots = slots_ref.shape[1]
    peers = out_ref.shape[0] // CAPD

    def clear(i, carry):
        out_ref[i, :TILE_ROWS, :] = jnp.zeros((TILE_ROWS, LANES), jnp.float32)
        out_ref[i, TILE_ROWS:, :] = jnp.full((8, LANES), -1.0, jnp.float32)
        return carry

    lax.fori_loop(0, peers * CAPD, clear, 0)

    def reset(i, carry):
        count_ref[i] = 0
        return carry

    lax.fori_loop(0, peers, reset, 0)

    def place(i, carry):
        entry = slots_ref[0, i]
        peer = entry // gshare
        rank = count_ref[peer]
        count_ref[peer] = rank + 1
        target = peer * CAPD + rank
        target_ref[i] = target
        out_ref[target, TILE_ROWS:, :] = jnp.full((8, LANES), (entry - peer * gshare).astype(jnp.float32))
        return carry

    lax.fori_loop(0, n_slots, place, 0)

    low_iota = lax.broadcasted_iota(jnp.int32, (LANES, LANES), 1).astype(jnp.float32)
    high_iota = lax.broadcasted_iota(jnp.int32, (PIX_ROWS, LANES), 0).astype(jnp.float32).astype(jnp.bfloat16)
    zero = jnp.bfloat16(0.0)
    blank = jnp.zeros((LANES, LANES), jnp.bfloat16)

    def prepare(s, carry):
        lanes = pl.ds(pl.multiple_of(s * LANES, LANES), LANES)
        for c in range(3):
            value = stream_ref[s, c]
            high = value.astype(jnp.bfloat16).astype(jnp.float32)
            rows_ref[s, c] = high
            rows_ref[s, 3 + c] = value - high
        pix = pix_ref[0, :, lanes]
        rows_ref[s, 6] = (pix >> 7).astype(jnp.float32)
        rows_ref[s, 7] = (pix & (LANES - 1)).astype(jnp.float32)
        return carry

    lax.fori_loop(0, strips, prepare, 0, unroll=4)

    def wide(s, i, d):
        return jnp.broadcast_to(rows_ref[s, i, d : d + 1, :], (16, LANES)).astype(jnp.bfloat16)

    def strip(s, carry):
        lows = jnp.transpose(rows_ref[s, 7])
        for d0 in range(0, dets, 2):
            rows, spreads = [], []
            for d in (d0, d0 + 1):
                hit = high_iota == wide(s, 6, d)
                rows.append(jnp.concatenate([jnp.where(hit, wide(s, i, d), zero) for i in range(6)], axis=0))
                low = jnp.broadcast_to(lows[:, d : d + 1], (LANES, LANES))
                spreads.append(jnp.where(low_iota == low, 1.0, 0.0).astype(jnp.bfloat16))
            spread = jnp.concatenate([
                jnp.concatenate([spreads[0], blank], axis=1), jnp.concatenate([blank, spreads[1]], axis=1)], axis=0)
            both = lax.dot_general(jnp.concatenate(rows, axis=1), spread, (((1,), (0,)), ((), ())),
                                   preferred_element_type=jnp.float32)
            both = both[:TILE_ROWS] + both[TILE_ROWS:]
            for d in (d0, d0 + 1):
                target = target_ref[tile_ref[0, d, s]]
                out_ref[target, :TILE_ROWS, :] += both[:, (d - d0) * LANES : (d - d0 + 1) * LANES]
        return carry

    lax.fori_loop(0, strips, strip, 0)


def gather_kernel(n, n_tm, tiles_ref, home_ref, owned_ref, got_ref, block_ref, homes_ref, det_sems, tm_sems):
    me, me_tm = lax.axis_index("det"), lax.axis_index("tm")
    gshare = home_ref.shape[1]
    barrier = pltpu.get_barrier_semaphore()
    for o in range(1, n):
        pl.semaphore_signal(barrier, inc=1, device_id={"det": lax.rem(me + o, n)}, device_id_type=pl.DeviceIdType.MESH)
    for o in range(1, n_tm):
        pl.semaphore_signal(barrier, inc=1, device_id={"tm": lax.rem(me_tm + o, n_tm)}, device_id_type=pl.DeviceIdType.MESH)
    pl.semaphore_wait(barrier, n + n_tm - 2)
    copies = []
    for o in range(1, n):
        peer = lax.rem(me + o, n)
        copy = remote(tiles_ref.at[pl.ds(peer * CAPD, CAPD)], got_ref.at[o], det_sems.at[0, o], det_sems.at[1, o],
                      {"det": peer})
        copy.start()
        copies.append(copy)
    got_ref[0] = tiles_ref[pl.ds(me * CAPD, CAPD)]
    for o in range(n):
        if o > 0:
            copies[o - 1].wait()
        for e in range(gshare):
            total = None if o == 0 else block_ref[e]
            for i in range(CAPD):
                label = got_ref[o, i, TILE_ROWS : TILE_ROWS + 1, :]
                term = jnp.where(label == float(e), got_ref[o, i, :TILE_ROWS, :], 0.0)
                total = term if total is None else total + term
            block_ref[e] = total
    codes = [jnp.full((1, LANES), home_ref[0, e], jnp.int32) for e in range(gshare)]
    owners = [code // OWN for code in codes]
    places = [code - owner * OWN for code, owner in zip(codes, owners)]
    ranks = []
    for e in range(gshare):
        rank = jnp.zeros((1, LANES), jnp.int32)
        for f in range(e):
            rank = rank + jnp.where(owners[f] == owners[e], 1, 0)
        ranks.append(rank)
    for peer in range(n_tm):
        for rank in range(CAPT):
            tile = jnp.zeros((TILE_ROWS, LANES), jnp.float32)
            label = jnp.full((1, LANES), -1, jnp.int32)
            for e in range(gshare):
                hit = jnp.where(owners[e] * CAPT + ranks[e] == peer * CAPT + rank, 1, 0)
                tile = jnp.where(hit == 1, block_ref[e], tile)
                label = jnp.where(hit == 1, places[e], label)
            homes_ref[peer * CAPT + rank, :TILE_ROWS, :] = tile
            homes_ref[peer * CAPT + rank, TILE_ROWS:, :] = jnp.broadcast_to(label.astype(jnp.float32), (8, LANES))
    copies = []
    for o in range(1, n_tm):
        peer = lax.rem(me_tm + o, n_tm)
        copy = remote(homes_ref.at[pl.ds(peer * CAPT, CAPT)], owned_ref.at[o], tm_sems.at[0, o], tm_sems.at[1, o],
                      {"tm": peer})
        copy.start()
        copies.append(copy)
    owned_ref[0] = homes_ref[pl.ds(me_tm * CAPT, CAPT)]
    for copy in copies:
        copy.wait()


def place_kernel(owned_ref, out_ref):
    n_tm = owned_ref.shape[0]
    for t in range(OWN):
        for c in range(3):
            total = jnp.zeros((PIX_ROWS, LANES), jnp.float32)
            for o in range(n_tm):
                for i in range(CAPT):
                    label = owned_ref[o, i, TILE_ROWS : TILE_ROWS + 1, :]
                    part = owned_ref[o, i, c * PIX_ROWS : (c + 1) * PIX_ROWS, :]
                    total = total + jnp.where(label == float(t), part, 0.0)
            for h in range(PIX_ROWS):
                out_ref[c, t : t + 1, h * LANES : (h + 1) * LANES] = total[h : h + 1, :]


def per_device(timestream, polar_angle, pixel_index, strip_tile, time_const, knee_freq, noise_slope,
               white_weight, mode_mix, coupling, device_slots, slot_home):
    dets, total = timestream.shape[1:]
    scans = total // SAMPLES
    n_det, n_tm = lax.axis_size("det"), lax.axis_size("tm")
    matrices, rows = transform_tables()
    matrices, rows = jnp.asarray(matrices), jnp.asarray(rows)
    blocks = 2 * HALF
    share = blocks // n_det
    f32 = jnp.float32
    vmem = pl.BlockSpec(memory_space=pltpu.VMEM)
    smem = pl.BlockSpec(memory_space=pltpu.SMEM)
    stream = pl.pallas_call(
        functools.partial(clean_kernel, n_det),
        out_shape=jax.ShapeDtypeStruct((scans * OUTER, 3, dets, LANES), f32),
        in_specs=[vmem] * 10,
        out_specs=vmem,
        scratch_shapes=[
            pltpu.VMEM((scans, blocks, dets, LANES), f32),
            pltpu.VMEM((scans, blocks, dets, LANES), f32),
            pltpu.VMEM((HALF + 1, dets, LANES), f32),
            pltpu.VMEM((HALF + 1, dets, LANES), f32),
            pltpu.VMEM((HALF * dets, 2 * LANES), f32),
            pltpu.VMEM((scans * OUTER, 2, dets, LANES), f32),
            pltpu.VMEM((dets, LANES), f32),
            pltpu.VMEM((n_det, dets, LANES), f32),
            pltpu.VMEM((scans, n_det, share, dets, LANES), f32),
            pltpu.VMEM((scans, n_det, share, dets, LANES), f32),
            pltpu.SemaphoreType.DMA((2, n_det)),
            pltpu.SemaphoreType.DMA((2, scans, n_det)),
            pltpu.SemaphoreType.DMA((2, scans, n_det)),
        ],
        compiler_params=pltpu.CompilerParams(vmem_limit_bytes=VMEM_LIMIT, collective_id=1, has_side_effects=True),
        name="clean",
    )(timestream, polar_angle, time_const, knee_freq, noise_slope, white_weight, mode_mix, coupling, matrices, rows)
    tiles = pl.pallas_call(
        functools.partial(bin_kernel, slot_home.shape[1]),
        out_shape=jax.ShapeDtypeStruct((n_det * CAPD, SLOT_ROWS, LANES), f32),
        in_specs=[vmem] * 2 + [smem] * 2,
        out_specs=vmem,
        scratch_shapes=[pltpu.VMEM((scans * OUTER, 8, dets, LANES), f32), pltpu.SMEM((device_slots.shape[1],), jnp.int32), pltpu.SMEM((n_det,), jnp.int32)],
        compiler_params=pltpu.CompilerParams(vmem_limit_bytes=VMEM_LIMIT),
        name="binning",
    )(stream, pixel_index, strip_tile, device_slots)
    owned = pl.pallas_call(
        functools.partial(gather_kernel, n_det, n_tm),
        out_shape=jax.ShapeDtypeStruct((n_tm, CAPT, SLOT_ROWS, LANES), f32),
        in_specs=[vmem, smem],
        out_specs=vmem,
        scratch_shapes=[
            pltpu.VMEM((n_det, CAPD, SLOT_ROWS, LANES), f32),
            pltpu.VMEM((slot_home.shape[1], TILE_ROWS, LANES), f32),
            pltpu.VMEM((n_tm * CAPT, SLOT_ROWS, LANES), f32),
            pltpu.SemaphoreType.DMA((2, n_det)),
            pltpu.SemaphoreType.DMA((2, n_tm)),
        ],
        compiler_params=pltpu.CompilerParams(vmem_limit_bytes=VMEM_LIMIT, collective_id=2, has_side_effects=True),
        name="gather",
    )(tiles, slot_home)
    out = pl.pallas_call(
        place_kernel,
        out_shape=jax.ShapeDtypeStruct((3, OWN, TILE_PIX), f32),
        in_specs=[vmem],
        out_specs=vmem,
        compiler_params=pltpu.CompilerParams(vmem_limit_bytes=VMEM_LIMIT),
        name="place",
    )(owned)
    return jnp.transpose(out, (1, 0, 2))


def solution(mesh):
    placed = (
        P("tm", "det", None),
        P("tm", "det", None),
        P("tm", "det", None),
        P("tm", "det", None),
        P("tm", "det"),
        P("tm", "det"),
        P("tm", "det"),
        P("tm", "det"),
        P("tm", "det", None),
        P(),
        P("tm", "det"),
        P("tm", "det"),
    )
    return jax.shard_map(
        per_device,
        mesh=mesh,
        in_specs=placed,
        out_specs=P(("tm", "det"), None, None),
        check_vma=False,
    )
```
